32 devices in a mesh: grp: 2 (over x), pop: 2 (over core), mp: 8 (over z, y).
Axes of the slice: x: 2, y: 2, z: 4, core: 2. Of those that a mesh axis runs over, the one named last changes fastest.
Arguments:
- token_ids: int32 [1024, 2], P('grp'), parts along dimension 0, may hold values from 0 to 32767
- ranks: int32 [1024], P(('grp', 'pop')), parts along dimension 0, may hold values from 0 to 511, each once
- embedding: bfloat16 [32768, 4096], P('pop', 'mp'), may hold values from -6 to 6
- mix_key: float32 [4096], P('mp'), may hold values from 0.05 to 0.95
- key_weight: bfloat16 [4096, 16384], P('pop', 'mp'), may hold values from -6 to 6
- value_weight: bfloat16 [16384, 4096], P('mp', 'pop'), may hold values from -6 to 6
- key_left: bfloat16 [1024, 4096], P(('grp', 'pop'), 'mp'), parts along dimension 0, may hold values from -6 to 6
- key_right: bfloat16 [1024, 16384], P(('grp', 'pop'), 'mp'), parts along dimension 0, may hold values from -6 to 6
- value_left: bfloat16 [1024, 16384], P(('grp', 'pop'), 'mp'), parts along dimension 0, may hold values from -6 to 6
- value_right: bfloat16 [1024, 4096], P(('grp', 'pop'), 'mp'), parts along dimension 0, may hold values from -6 to 6
Outputs:
- mixed: bfloat16 [2048, 4096], P(('grp', 'pop'), 'mp'), parts along dimension 0
- new_key: bfloat16 [8192, 16384], P(('grp', 'pop'), 'mp'), parts along dimension 0
- new_value: bfloat16 [32768, 4096], P(('grp', 'mp'), 'pop'), parts along dimension 0
The draws below stay inside these ranges and needn't reach their ends.
There are 2 independent parts, one for each index of `grp`. The reference program is written for one: setup_inputs(seed, part) draws one part's arguments, and reference() takes and returns one part's arrays. A program takes and returns all parts, laid end to end along the dimension named above; an argument that names none is the same for every part. Nothing has to cross between parts.
Inputs may be any that keep to these rules, and one draw needn't show every extreme that they name: `ranks`: each member's rank; every rank appears exactly once in a run. `token_ids`: token ids index the embedding table.
All inputs are finite; a program needn't handle non-finite values.
Results may differ from the reference program's by a relative error of at most 0.006.
Values may be sent and summed in bfloat16 or wider, within the bound.
A program may use at most 320 MiB of HBM per device.

```python
import math
import jax
import jax.numpy as jnp
import numpy as np

D = 4096
FF = 16384
VOCAB = 32768
POP = 512
TOKENS = 1024


def with_ends(entries, own_key, least, high):
    longest = entries.shape.index(max(entries.shape))
    spots = []
    for shift in (0, 1):
        where = [jax.random.randint(jax.random.fold_in(own_key, axis), (), 0, length) for axis, length in enumerate(entries.shape)]
        where[longest] = (where[longest] + shift) % entries.shape[longest]
        spots.append(tuple(where))
    return entries.at[spots[0]].set(least).at[spots[1]].set(high)


def raised(values, own_key, source, target, shards_of, factor):
    def block_of(axis_at):
        return (jnp.arange(values.shape[axis_at]) // (values.shape[axis_at] // shards_of)).reshape((-1,) + (1,) * (values.ndim - 1 - axis_at))

    near = jax.random.permutation(own_key, shards_of)[block_of(target)]
    other_side = (block_of(target) + shards_of // 2) % shards_of
    return jnp.where((block_of(source) == near) | (block_of(source) == other_side), factor * values, values)


def block_scale(own_key, shape, cuts, least, high):
    factor_of, own = 1.0, jax.random.fold_in(own_key, 6)
    for axis_at, blocks in cuts:
        heights = jnp.exp(jax.random.uniform(jax.random.fold_in(own, axis_at), (blocks,), jnp.float32, least / len(cuts), high / len(cuts)))
        factor_of = factor_of * jnp.repeat(heights, shape[axis_at] // blocks).reshape([-1 if axis == axis_at else 1 for axis in range(len(shape))])
    return factor_of


def rank_table(count, lean):
    portions = [(1 << 20) // math.isqrt(grade ** lean) + 1 for grade in range(1, count + 1)]
    scale = 1 + sum(portions) // (1 << 30)
    return np.cumsum(np.array([max(1, weight // scale) for weight in portions]))


def ranked_ids(rng, extent, number_of, slope):
    listing = rank_table(number_of, slope)
    lot = jax.random.randint(jax.random.fold_in(rng, 1), extent, 0, int(listing[number_of - 1]))
    grade = jnp.searchsorted(jnp.asarray(listing, jnp.int32), lot, side="right")
    return jax.random.permutation(jax.random.fold_in(rng, 2), number_of)[grade].astype(jnp.int32)


def scatter_about(rng, dims, scale, most, shards=(), kind=jnp.bfloat16):
    result = jax.random.normal(rng, dims, jnp.float32) * scale
    if len(shards) > 0:
        result = block_scale(rng, dims, shards, -0.22, 0.18) * result
    return jnp.clip(result, min=-most, max=most).astype(kind)


def gaussian_with(own_key, extent, width, most, cuts, heavy, kind=jnp.bfloat16):
    entries = width * jax.random.normal(own_key, extent, jnp.float32)
    if cuts:
        entries = entries * block_scale(own_key, extent, cuts, -0.22, 0.18)
    return jnp.clip(raised(entries, jax.random.fold_in(own_key, 3), *heavy), -most, most).astype(kind)


def setup_inputs(seed: int = 0, part: int = 0) -> dict:
    seeds = jax.random.split(jax.random.key(seed), 11)
    own_keys = jax.random.split(jax.random.fold_in(seeds[10], part), 11)
    return {
        "token_ids": with_ends(ranked_ids(own_keys[0], (POP, 2), VOCAB, 2), jax.random.fold_in(own_keys[0], 3), 0, VOCAB - 1).astype(jnp.int32),
        "ranks": jax.random.permutation(own_keys[1], POP).astype(jnp.int32),
        "embedding": scatter_about(seeds[2], (VOCAB, D), 1.0, 6.0, ((0, 2), (1, 8))),
        "mix_key": jnp.clip(0.05 + 0.9 * jax.random.uniform(seeds[3], (D,), jnp.float32) ** block_scale(seeds[3], (D,), ((0, 8),), -0.2, 0.2), 0.05, 0.95),
        "key_weight": scatter_about(seeds[4], (D, FF), 1.0, 6.0, ((0, 2), (1, 8))),
        "value_weight": gaussian_with(seeds[5], (FF, D), 1.0, 6.0, ((0, 8), (1, 2)), (0, 1, 8, 2.0)),
        "key_left": scatter_about(own_keys[6], (POP, D), 1.0, 6.0, ((0, 2), (1, 8))),
        "key_right": scatter_about(own_keys[7], (POP, FF), 1.0, 6.0, ((0, 2), (1, 8))),
        "value_left": scatter_about(own_keys[8], (POP, FF), 1.0, 6.0, ((0, 2), (1, 8))),
        "value_right": scatter_about(own_keys[9], (POP, D), 1.0, 6.0, ((0, 2), (1, 8))),
    }


noise_scale = 0.5
step_scale = 8.0


def reference(token_ids, ranks, embedding, mix_key, key_weight, value_weight, key_left, key_right, value_left, value_right):
    inv_model = D ** -0.5
    inv_hidden = FF ** -0.5
    rows = embedding[token_ids].astype(jnp.float32)
    before = jnp.concatenate([jnp.zeros((POP, 1, D), jnp.float32), rows[:, :1]], axis=1)
    keyed = (rows + (before - rows) * mix_key).astype(jnp.bfloat16)
    projected = jnp.dot(keyed.reshape(TOKENS, D), key_weight, preferred_element_type=jnp.float32)
    inner_key = jnp.einsum("mtd,md->mt", keyed.astype(jnp.float32), key_left.astype(jnp.float32))
    hidden = projected.reshape(POP, 2, FF) * inv_model + (noise_scale * inv_model) * inner_key[:, :, None] * key_right.astype(jnp.float32)[:, None, :]
    squared = (jnp.maximum(hidden, 0.0) ** 2).astype(jnp.bfloat16)
    inner_value = jnp.einsum("mtf,mf->mt", squared.astype(jnp.float32), value_left.astype(jnp.float32))
    direct = jnp.dot(squared.reshape(TOKENS, FF), value_weight, preferred_element_type=jnp.float32).reshape(POP, 2, D)
    mixed = ((direct + noise_scale * inner_value[:, :, None] * value_right.astype(jnp.float32)[:, None, :]) * inv_hidden).astype(jnp.bfloat16)
    fitness = (2 * ranks - (POP - 1)).astype(jnp.float32) / (POP - 1)
    scaled_right = (fitness[:, None] * key_right.astype(jnp.float32)).astype(jnp.bfloat16)
    scaled_left = (fitness[:, None] * value_left.astype(jnp.float32)).astype(jnp.bfloat16)
    key_grad = jnp.dot(key_left.T, scaled_right, preferred_element_type=jnp.float32)
    value_grad = jnp.dot(scaled_left.T, value_right, preferred_element_type=jnp.float32)
    new_key = (key_weight.astype(jnp.float32) + (step_scale / POP) * key_grad).astype(jnp.bfloat16)
    new_value = (value_weight.astype(jnp.float32) + (step_scale / POP) * value_grad).astype(jnp.bfloat16)
    return mixed.reshape(TOKENS, D), new_key, new_value
```

```python
import functools

import jax
import jax.numpy as jnp
from jax import lax
from jax.experimental import pallas as pl
from jax.experimental.pallas import tpu as pltpu
from jax.sharding import PartitionSpec as P

noise_scale = 0.5
step_scale = 8.0
vmem_bytes = 58 * 1024 * 1024
pad_rows = 16


def dot(left, right):
    return jnp.dot(left, right, preferred_element_type=jnp.float32)


def contract_first(left, right):
    return lax.dot_general(
        left, right, (((0,), (0,)), ((), ())), preferred_element_type=jnp.float32
    )


def forward_kernel(
    inv_model, inv_hidden, side_ref, keyed_ref, key_own, key_peer, value_own, value_peer,
    key_right, value_left, value_right, out_ref, total, inner_key, inner_value,
):
    step, last = pl.program_id(0), pl.num_programs(0) - 1
    slices, padded, width = keyed_ref.shape
    tokens, half = padded - pad_rows, slices // 2
    tile = key_own.shape[1]
    mine = side_ref[0] * half
    theirs = half - mine

    @pl.when(step == 0)
    def _():
        groups = tokens // width
        line = lax.broadcasted_iota(jnp.int32, (pad_rows, 128), 0)
        for g in range(groups):
            chosen = (line < 3 * groups) & (line % groups == g)
            ones = jnp.where(chosen, 1.0, 0.0).astype(jnp.bfloat16)
            partial = jnp.zeros((width, 128), jnp.float32)
            for s in range(slices):
                partial += contract_first(keyed_ref[s, tokens:, :], ones)
            inner_key[g * width : (g + 1) * width, :] = partial * (noise_scale * inv_model)
        inner_value[...] = jnp.zeros_like(inner_value)

    projected = jnp.zeros((tokens, tile), jnp.float32)
    for j in range(half):
        rows = slice(j * width, (j + 1) * width)
        projected += dot(keyed_ref[mine + j, :tokens, :], key_own[rows, :])
        projected += dot(keyed_ref[theirs + j, :tokens, :], key_peer[rows, :])
    right = key_right[...].astype(jnp.float32)
    left = value_left[...].astype(jnp.float32)
    members = right.shape[0]
    parts = []
    for t in range(tokens // members):
        own = slice(t * members, (t + 1) * members)
        pieces = []
        for c in range(0, tile, 128):
            cols = slice(c, c + 128)
            hidden = projected[own, cols] * inv_model + inner_key[own, :] * right[:, cols]
            rounded = (jnp.maximum(hidden, 0.0) ** 2).astype(jnp.bfloat16)
            inner_value[own, :] += rounded.astype(jnp.float32) * left[:, cols]
            pieces.append(rounded)
        parts.append(jnp.concatenate(pieces, axis=1))
    squared = jnp.concatenate(parts, axis=0)

    for j in range(half):
        cols = slice(j * width, (j + 1) * width)
        for base, weight in ((mine, value_own), (theirs, value_peer)):
            product = dot(squared, weight[:, cols])

            @pl.when(step == 0)
            def _():
                total[base + j] = product

            @pl.when(step > 0)
            def _():
                total[base + j] += product

    @pl.when(step == last)
    def _():
        amount = noise_scale * jnp.sum(inner_value[...], axis=1, keepdims=True)
        for s in range(slices):
            spread = value_right[s].astype(jnp.float32)
            for t in range(tokens // members):
                own = slice(t * members, (t + 1) * members)
                out_ref[s, own, :] = (
                    (total[s, own, :] + amount[own, :] * spread) * inv_hidden
                ).astype(jnp.bfloat16)


def forward(side, keyed, key_own, key_peer, value_own, value_peer, key_right, value_left,
            value_right, inv_model, inv_hidden):
    slices, padded, width = keyed.shape
    tokens = padded - pad_rows
    rows, hidden = key_own.shape
    members = key_right.shape[0]
    tile = min(512, hidden)
    whole = lambda i, s: (0, 0, 0)
    column = lambda i, s: (0, i)
    row = lambda i, s: (i, 0)
    return pl.pallas_call(
        functools.partial(forward_kernel, inv_model, inv_hidden),
        out_shape=jax.ShapeDtypeStruct((slices, tokens, width), jnp.bfloat16),
        grid_spec=pltpu.PrefetchScalarGridSpec(
            num_scalar_prefetch=1,
            grid=(hidden // tile,),
            in_specs=[
                pl.BlockSpec(keyed.shape, whole),
                pl.BlockSpec((rows, tile), column),
                pl.BlockSpec((rows, tile), column),
                pl.BlockSpec((tile, rows), row),
                pl.BlockSpec((tile, rows), row),
                pl.BlockSpec((members, tile), column),
                pl.BlockSpec((members, tile), column),
                pl.BlockSpec(value_right.shape, whole),
            ],
            out_specs=pl.BlockSpec((slices, tokens, width), whole),
            scratch_shapes=[
                pltpu.VMEM((slices, tokens, width), jnp.float32),
                pltpu.VMEM((tokens, 128), jnp.float32),
                pltpu.VMEM((tokens, 128), jnp.float32),
            ],
        ),
        compiler_params=pltpu.CompilerParams(vmem_limit_bytes=vmem_bytes),
        cost_estimate=pl.CostEstimate(
            flops=8 * tokens * rows * hidden,
            bytes_accessed=8 * rows * hidden + 4 * tokens * slices * width,
            transcendentals=0,
        ),
        name="forward",
    )(side, keyed, key_own, key_peer, value_own, value_peer, key_right, value_left, value_right)


def key_step_kernel(step, side_ref, left_own, left_peer, right_own, right_peer, weight, out_ref):
    columns = out_ref.shape[1]
    chunk = min(512, columns)
    own, peer = left_own[0], left_peer[0]
    for c in range(0, columns, chunk):
        cols = slice(c, c + chunk)
        grad = contract_first(own, right_own[:, cols]) + contract_first(peer, right_peer[:, cols])
        out_ref[:, cols] = (weight[:, cols].astype(jnp.float32) + step * grad).astype(jnp.bfloat16)


def key_step(side, left_all, left_peer, right_own, right_peer, weight, step):
    half, members, width = left_peer.shape
    rows, columns = weight.shape
    fixed = pl.BlockSpec((members, columns), lambda j, s: (0, 0))
    tile = pl.BlockSpec((width, columns), lambda j, s: (j, 0))
    return pl.pallas_call(
        functools.partial(key_step_kernel, step),
        out_shape=jax.ShapeDtypeStruct(weight.shape, jnp.bfloat16),
        grid_spec=pltpu.PrefetchScalarGridSpec(
            num_scalar_prefetch=1,
            grid=(half,),
            in_specs=[
                pl.BlockSpec((1, members, width), lambda j, s: (s[0] * half + j, 0, 0)),
                pl.BlockSpec((1, members, width), lambda j, s: (j, 0, 0)),
                fixed,
                fixed,
                tile,
            ],
            out_specs=tile,
        ),
        compiler_params=pltpu.CompilerParams(vmem_limit_bytes=vmem_bytes),
        cost_estimate=pl.CostEstimate(
            flops=4 * members * rows * columns,
            bytes_accessed=4 * rows * columns + 4 * members * (rows + columns),
            transcendentals=0,
        ),
        name="key_step",
    )(side, left_all, left_peer, right_own, right_peer, weight)


def value_step_kernel(step, side_ref, left_own, left_peer, right_all, right_peer, weight, out_ref):
    half, _, width = right_peer.shape
    mine = side_ref[0] * half
    own, peer = left_own[...], left_peer[...]
    for j in range(half):
        cols = slice(j * width, (j + 1) * width)
        grad = contract_first(own, right_all[mine + j]) + contract_first(peer, right_peer[j])
        out_ref[:, cols] = (weight[:, cols].astype(jnp.float32) + step * grad).astype(jnp.bfloat16)


def value_step(side, left_own, left_peer, right_all, right_peer, weight, step):
    half, members, width = right_peer.shape
    rows, columns = weight.shape
    size = min(512, rows)
    side_tile = pl.BlockSpec((members, size), lambda i, s: (0, i))
    tile = pl.BlockSpec((size, columns), lambda i, s: (i, 0))
    return pl.pallas_call(
        functools.partial(value_step_kernel, step),
        out_shape=jax.ShapeDtypeStruct(weight.shape, jnp.bfloat16),
        grid_spec=pltpu.PrefetchScalarGridSpec(
            num_scalar_prefetch=1,
            grid=(rows // size,),
            in_specs=[
                side_tile,
                side_tile,
                pl.BlockSpec(right_all.shape, lambda i, s: (0, 0, 0)),
                pl.BlockSpec(right_peer.shape, lambda i, s: (0, 0, 0)),
                tile,
            ],
            out_specs=tile,
        ),
        compiler_params=pltpu.CompilerParams(vmem_limit_bytes=vmem_bytes),
        cost_estimate=pl.CostEstimate(
            flops=4 * members * rows * columns,
            bytes_accessed=4 * rows * columns + 4 * members * (rows + columns),
            transcendentals=0,
        ),
        name="value_step",
    )(side, left_own, left_peer, right_all, right_peer, weight)


def shards(
    token_ids, ranks, embedding, mix_key, key_weight, value_weight,
    key_left, key_right, value_left, value_right,
):
    members = ranks.shape[0]
    population = members * lax.axis_size("pop")
    side = lax.axis_index("pop")
    side_ref = side.astype(jnp.int32).reshape(1)
    slices = lax.axis_size("mp")
    half = slices // 2
    width = embedding.shape[1]
    model = slices * width
    hidden = slices * key_weight.shape[1]
    swap = lambda array: lax.ppermute(array, "pop", [(0, 1), (1, 0)])

    half_vocab = embedding.shape[0]
    by_side = jnp.swapaxes(token_ids.reshape(2, members, 2), 1, 2)

    def look(which):
        ids = lax.dynamic_index_in_dim(by_side, which, 0, keepdims=False).reshape(-1)
        ids = ids - side * half_vocab
        inside = (ids >= 0) & (ids < half_vocab)
        return jnp.take(embedding, jnp.clip(ids, 0, half_vocab - 1), axis=0, mode="clip"), inside

    theirs, _ = look(1 - side)
    received = swap(theirs)
    mine, inside = look(side)
    rows = jnp.where(inside[:, None], mine, received).astype(jnp.float32)
    first, second = rows[:members], rows[members:]
    keyed = jnp.concatenate(
        [first + (0.0 - first) * mix_key, second + (first - second) * mix_key], axis=0
    ).astype(jnp.bfloat16)
    left = key_left.astype(jnp.float32)
    inner = jnp.sum(
        keyed.astype(jnp.float32).reshape(2, members, width) * left[None], axis=2
    ).reshape(-1)
    high = inner.astype(jnp.bfloat16)
    rest = inner - high.astype(jnp.float32)
    middle = rest.astype(jnp.bfloat16)
    low = (rest - middle.astype(jnp.float32)).astype(jnp.bfloat16)
    groups = -(-2 * members // width)
    tail = jnp.stack([high, middle, low]).reshape(3 * groups, width)
    tail = jnp.pad(tail, ((0, pad_rows - 3 * groups), (0, 0)))
    keyed_all = lax.all_gather(jnp.concatenate([keyed, tail], axis=0), "mp", axis=0)
    right_all = lax.all_gather(value_right, "mp", axis=0)
    left_all = lax.all_gather(key_left, "mp", axis=0)

    key_peer, value_peer = swap(key_weight), swap(value_weight)
    partial = forward(
        side_ref, keyed_all, key_weight, key_peer, value_weight, value_peer,
        key_right, value_left, right_all, model ** -0.5, hidden ** -0.5,
    )
    mixed = lax.psum_scatter(partial, "mp", scatter_dimension=0, tiled=False)
    mixed = jnp.swapaxes(mixed.reshape(2, members, width), 0, 1).reshape(2 * members, width)

    fitness = (2 * ranks - (population - 1)).astype(jnp.float32) / (population - 1)
    scaled_right = (fitness[:, None] * key_right.astype(jnp.float32)).astype(jnp.bfloat16)
    scaled_left = (fitness[:, None] * value_left.astype(jnp.float32)).astype(jnp.bfloat16)
    other = (1 - side) * half
    left_peer = swap(lax.dynamic_slice_in_dim(left_all, other, half, 0))
    right_peer = swap(lax.dynamic_slice_in_dim(right_all, other, half, 0))
    step = step_scale / population
    new_key = key_step(
        side_ref, left_all, left_peer, scaled_right, swap(scaled_right), key_weight, step
    )
    new_value = value_step(
        side_ref, scaled_left, swap(scaled_left), right_all, right_peer, value_weight, step
    )
    return (mixed, new_key, new_value)


def solution(mesh):
    placed = (
        P("grp", None),
        P(("grp", "pop")),
        P("pop", "mp"),
        P("mp"),
        P("pop", "mp"),
        P("mp", "pop"),
        P(("grp", "pop"), "mp"),
        P(("grp", "pop"), "mp"),
        P(("grp", "pop"), "mp"),
        P(("grp", "pop"), "mp"),
    )
    return jax.shard_map(
        shards,
        mesh=mesh,
        in_specs=placed,
        out_specs=(P(("grp", "pop"), "mp"), P(("grp", "pop"), "mp"), P(("grp", "mp"), "pop")),
        check_vma=False,
    )
```

```python
import functools

import jax
import jax.numpy as jnp
from jax import lax
from jax.experimental import pallas as pl
from jax.experimental.pallas import tpu as pltpu
from jax.sharding import PartitionSpec as P

noise_scale = 0.5
step_scale = 8.0
vmem_bytes = 58 * 1024 * 1024
pad_rows = 16


def dot(left, right):
    return jnp.dot(left, right, preferred_element_type=jnp.float32)


def contract_first(left, right):
    return lax.dot_general(
        left, right, (((0,), (0,)), ((), ())), preferred_element_type=jnp.float32
    )


def forward_kernel(
    inv_model, inv_hidden, side_ref, keyed_ref, key_own, key_peer, value_own, value_peer,
    key_right, value_left, value_right, out_ref, total, inner_key, inner_value,
):
    step, last = pl.program_id(0), pl.num_programs(0) - 1
    slices, padded, width = keyed_ref.shape
    tokens, half = padded - pad_rows, slices // 2
    tile = key_own.shape[1]
    mine = side_ref[0] * half
    theirs = half - mine

    @pl.when(step == 0)
    def _():
        groups = tokens // width
        line = lax.broadcasted_iota(jnp.int32, (pad_rows, 128), 0)
        for g in range(groups):
            chosen = (line < 3 * groups) & (line % groups == g)
            ones = jnp.where(chosen, 1.0, 0.0).astype(jnp.bfloat16)
            partial = jnp.zeros((width, 128), jnp.float32)
            for s in range(slices):
                partial += contract_first(keyed_ref[s, tokens:, :], ones)
            inner_key[g * width : (g + 1) * width, :] = partial * (noise_scale * inv_model)
        inner_value[...] = jnp.zeros_like(inner_value)

    projected = jnp.zeros((tokens, tile), jnp.float32)
    for j in range(half):
        rows = slice(j * width, (j + 1) * width)
        projected += dot(keyed_ref[mine + j, :tokens, :], key_own[rows, :])
        projected += dot(keyed_ref[theirs + j, :tokens, :], key_peer[rows, :])
    right = key_right[...].astype(jnp.float32)
    left = value_left[...].astype(jnp.float32)
    members = right.shape[0]
    parts = []
    for t in range(tokens // members):
        own = slice(t * members, (t + 1) * members)
        pieces = []
        for c in range(0, tile, 128):
            cols = slice(c, c + 128)
            hidden = projected[own, cols] * inv_model + inner_key[own, :] * right[:, cols]
            rounded = (jnp.maximum(hidden, 0.0) ** 2).astype(jnp.bfloat16)
            inner_value[own, :] += rounded.astype(jnp.float32) * left[:, cols]
            pieces.append(rounded)
        parts.append(jnp.concatenate(pieces, axis=1))
    squared = jnp.concatenate(parts, axis=0)

    for j in range(half):
        cols = slice(j * width, (j + 1) * width)
        for base, weight in ((mine, value_own), (theirs, value_peer)):
            product = dot(squared, weight[:, cols])

            @pl.when(step == 0)
            def _():
                total[base + j] = product

            @pl.when(step > 0)
            def _():
                total[base + j] += product

    @pl.when(step == last)
    def _():
        amount = noise_scale * jnp.sum(inner_value[...], axis=1, keepdims=True)
        for s in range(slices):
            spread = value_right[s].astype(jnp.float32)
            for t in range(tokens // members):
                own = slice(t * members, (t + 1) * members)
                out_ref[s, own, :] = (
                    (total[s, own, :] + amount[own, :] * spread) * inv_hidden
                ).astype(jnp.bfloat16)


def forward(side, keyed, key_own, key_peer, value_own, value_peer, key_right, value_left,
            value_right, inv_model, inv_hidden):
    slices, padded, width = keyed.shape
    tokens = padded - pad_rows
    rows, hidden = key_own.shape
    members = key_right.shape[0]
    tile = min(512, hidden)
    whole = lambda i, s: (0, 0, 0)
    column = lambda i, s: (0, i)
    row = lambda i, s: (i, 0)
    return pl.pallas_call(
        functools.partial(forward_kernel, inv_model, inv_hidden),
        out_shape=jax.ShapeDtypeStruct((slices, tokens, width), jnp.bfloat16),
        grid_spec=pltpu.PrefetchScalarGridSpec(
            num_scalar_prefetch=1,
            grid=(hidden // tile,),
            in_specs=[
                pl.BlockSpec(keyed.shape, whole),
                pl.BlockSpec((rows, tile), column),
                pl.BlockSpec((rows, tile), column),
                pl.BlockSpec((tile, rows), row),
                pl.BlockSpec((tile, rows), row),
                pl.BlockSpec((members, tile), column),
                pl.BlockSpec((members, tile), column),
                pl.BlockSpec(value_right.shape, whole),
            ],
            out_specs=pl.BlockSpec((slices, tokens, width), whole),
            scratch_shapes=[
                pltpu.VMEM((slices, tokens, width), jnp.float32),
                pltpu.VMEM((tokens, 128), jnp.float32),
                pltpu.VMEM((tokens, 128), jnp.float32),
            ],
        ),
        compiler_params=pltpu.CompilerParams(vmem_limit_bytes=vmem_bytes),
        cost_estimate=pl.CostEstimate(
            flops=8 * tokens * rows * hidden,
            bytes_accessed=8 * rows * hidden + 4 * tokens * slices * width,
            transcendentals=0,
        ),
        name="forward",
    )(side, keyed, key_own, key_peer, value_own, value_peer, key_right, value_left, value_right)


def coordinates():
    place = lax.axis_index("mp")
    return lax.div(place, 2), lax.rem(place, 2)


def pick(z, table):
    total = 0
    for value, row in enumerate(table):
        total = total + (1 - lax.div(lax.rem(z + 4 - value, 4) + 3, 4)) * row
    return total


def greet(z, y):
    barrier = pltpu.get_barrier_semaphore()

    def tell(zz, yy):
        pl.semaphore_signal(
            barrier, inc=1, device_id={"mp": 2 * zz + yy}, device_id_type=pl.DeviceIdType.MESH
        )

    tell(z, 1 - y)
    pl.when(z > 0)(lambda: tell(z - 1, y))
    pl.when(z < 3)(lambda: tell(z + 1, y))
    pl.semaphore_wait(barrier, 1 + lax.div(z + 3, 4) + lax.div(6 - z, 4))


def remote(source, target, send, recv, zz, yy):
    return pltpu.make_async_remote_copy(
        src_ref=source,
        dst_ref=target,
        send_sem=send,
        recv_sem=recv,
        device_id={"mp": 2 * zz + yy},
        device_id_type=pl.DeviceIdType.MESH,
    )


def split(row):
    high = row.astype(jnp.bfloat16)
    rest = row - high.astype(jnp.float32)
    middle = rest.astype(jnp.bfloat16)
    low = (rest - middle.astype(jnp.float32)).astype(jnp.bfloat16)
    return high, middle, low


def as_tail(row):
    line = lax.broadcasted_iota(jnp.int32, row.shape, 0)
    high, middle, low = [term.astype(jnp.float32) for term in split(row)]
    kept = jnp.where(line == 0, high, jnp.where(line == 1, middle, jnp.where(line == 2, low, 0.0)))
    return kept.astype(jnp.bfloat16)


def from_tail(tail):
    total = jnp.sum(tail.astype(jnp.float32), axis=0, keepdims=True)
    return jnp.broadcast_to(total, tail.shape)


gather_order = ((0, 1, 2, 3), (1, 0, 2, 3), (2, 3, 1, 0), (3, 2, 1, 0))
scatter_order = ((3, 2, 1, 0), (3, 0, 2, 1), (0, 3, 1, 2), (0, 1, 2, 3))


def gather_key_kernel(
    inv_model, keyed, key_own, key_peer, key_right, value_left, squared, inner_value,
    held, loaded, projected, inner_key, load_sem, right_sem, left_sem, across_sem, recv_sem,
):
    z, y = coordinates()
    side = lax.axis_index("pop")
    slices, padded, width = held.shape
    tokens, half = padded - pad_rows, slices // 2
    hidden = key_own.shape[1]
    members = key_right.shape[0]
    order = [pick(z, [row[k] for row in gather_order]) for k in range(4)]
    own = [2 * b + y for b in order]
    other = [2 * b + 1 - y for b in order]
    sequence = [own[0], own[1], other[0], own[2], other[1], own[3], other[2], other[3]]

    def load(k):
        block, slot = sequence[k], k % 2
        row = pl.multiple_of(lax.rem(block, half) * width, width)
        from_own = lax.div(block, half) == side

        @pl.when(from_own)
        def _():
            pltpu.make_async_copy(
                key_own.at[pl.ds(row, width), :], loaded.at[slot], load_sem.at[slot]
            ).start()

        @pl.when(jnp.logical_not(from_own))
        def _():
            pltpu.make_async_copy(
                key_peer.at[pl.ds(row, width), :], loaded.at[slot], load_sem.at[slot]
            ).start()

    load(0)
    held[own[0]] = keyed[...]
    greet(z, y)

    def go_right(b):
        block = held.at[2 * b + y]
        return remote(block, block, right_sem.at[b], recv_sem.at[2 * b + y], z + 1, y)

    def go_left(b):
        block = held.at[2 * b + y]
        return remote(block, block, left_sem.at[b], recv_sem.at[2 * b + y], z - 1, y)

    def go_across(b):
        block = held.at[2 * b + y]
        return remote(block, block, across_sem.at[b], recv_sem.at[2 * b + y], z, 1 - y)

    def arrived(block):
        pltpu.make_async_copy(held.at[block], held.at[block], recv_sem.at[block]).wait()

    def forward_on(k, act):
        b = order[k]
        pl.when((b <= z) & (z < 3))(lambda: act(go_right(b)))
        pl.when((b >= z) & (z > 0))(lambda: act(go_left(b)))
        act(go_across(b))

    ones = jnp.ones((pad_rows, 128), jnp.bfloat16)
    chunk = 512

    def compute(k):
        block, slot = sequence[k], k % 2
        if k + 1 < len(sequence):
            load(k + 1)
        pltpu.make_async_copy(
            key_own.at[pl.ds(0, width), :], loaded.at[slot], load_sem.at[slot]
        ).wait()
        partial = contract_first(held[block, tokens:, :], ones)
        inner_key[...] = partial if k == 0 else inner_key[...] + partial

        @pl.loop(0, hidden // chunk)
        def _(c):
            cols = pl.ds(pl.multiple_of(c * chunk, chunk), chunk)
            product = dot(held[block, :tokens, :], loaded[slot, :, cols])
            projected[:, cols] = product if k == 0 else projected[:, cols] + product

    k = 0
    for step in range(4):
        if step > 0:
            arrived(own[step])
        forward_on(step, lambda copy: copy.start())
        compute(k)
        k += 1
        if step > 0:
            arrived(other[step - 1])
            compute(k)
            k += 1
    arrived(other[3])
    compute(k)

    factor = inner_key[...] * (noise_scale * inv_model)
    inner_key[...] = factor
    inner_value[...] = jnp.zeros_like(inner_value)

    @pl.loop(0, hidden // 128)
    def _(c):
        cols = pl.ds(pl.multiple_of(c * 128, 128), 128)
        right = key_right[:, cols].astype(jnp.float32)
        left = value_left[:, cols].astype(jnp.float32)
        for t in range(tokens // members):
            rows = slice(t * members, (t + 1) * members)
            value = projected[rows, cols] * inv_model + inner_key[rows, :] * right
            rounded = (jnp.maximum(value, 0.0) ** 2).astype(jnp.bfloat16)
            squared[rows, cols] = rounded
            inner_value[rows, :] += rounded.astype(jnp.float32) * left

    for step in range(4):
        forward_on(step, lambda copy: copy.wait_send())


def gather_key(keyed, key_own, key_peer, key_right, value_left, inv_model):
    padded, width = keyed.shape
    tokens = padded - pad_rows
    hidden = key_own.shape[1]
    slices = 8
    vmem = pl.BlockSpec(memory_space=pltpu.VMEM)
    hbm = pl.BlockSpec(memory_space=pl.ANY)
    return pl.pallas_call(
        functools.partial(gather_key_kernel, inv_model),
        out_shape=(
            jax.ShapeDtypeStruct((tokens, hidden), jnp.bfloat16),
            jax.ShapeDtypeStruct((tokens, 128), jnp.float32),
        ),
        in_specs=[vmem, hbm, hbm, vmem, vmem],
        out_specs=(vmem, vmem),
        scratch_shapes=[
            pltpu.VMEM((slices, padded, width), jnp.bfloat16),
            pltpu.VMEM((2, width, hidden), jnp.bfloat16),
            pltpu.VMEM((tokens, hidden), jnp.float32),
            pltpu.VMEM((tokens, 128), jnp.float32),
            pltpu.SemaphoreType.DMA((2,)),
            pltpu.SemaphoreType.DMA((4,)),
            pltpu.SemaphoreType.DMA((4,)),
            pltpu.SemaphoreType.DMA((4,)),
            pltpu.SemaphoreType.DMA((slices,)),
        ],
        compiler_params=pltpu.CompilerParams(
            vmem_limit_bytes=vmem_bytes, collective_id=1, has_side_effects=True
        ),
        cost_estimate=pl.CostEstimate(
            flops=16 * tokens * width * hidden,
            bytes_accessed=16 * width * hidden,
            transcendentals=0,
        ),
        name="gather_key",
    )(keyed, key_own, key_peer, key_right, value_left)


def value_scatter_kernel(
    inv_hidden, squared, inner_value, value_own, value_peer, value_right, out,
    loaded, total, inner, across, from_across, to_right, to_left, from_left, from_right,
    load_sem, across_sem, across_recv, right_sem, left_sem, left_recv, right_recv,
):
    z, y = coordinates()
    side = lax.axis_index("pop")
    rows, width = loaded.shape[1], loaded.shape[2]
    tokens = squared.shape[0]
    members = value_right.shape[0]
    half = 4
    order = [pick(z, [row[k] for row in scatter_order]) for k in range(4)]
    sequence = []
    for t in order:
        sequence += [2 * t + 1 - y, 2 * t + y]

    def load(k):
        block, slot = sequence[k], k % 2
        column = pl.multiple_of(lax.rem(block, half) * width, width)
        from_own = lax.div(block, half) == side

        @pl.when(from_own)
        def _():
            pltpu.make_async_copy(
                value_own.at[:, pl.ds(column, width)], loaded.at[slot], load_sem.at[slot]
            ).start()

        @pl.when(jnp.logical_not(from_own))
        def _():
            pltpu.make_async_copy(
                value_peer.at[:, pl.ds(column, width)], loaded.at[slot], load_sem.at[slot]
            ).start()

    load(0)
    greet(z, y)
    ones = jnp.ones((pad_rows, 128), jnp.bfloat16)
    row = jnp.zeros((pad_rows, tokens), jnp.float32)
    for term in split(inner_value[...]):
        row += lax.dot_general(
            ones, term, (((1,), (1,)), ((), ())), preferred_element_type=jnp.float32
        )

    def go_across(t):
        return remote(
            across.at[t], from_across.at[t], across_sem.at[t], across_recv.at[t], z, 1 - y
        )

    def go_right(t):
        return remote(
            to_right.at[t], from_left.at[t], right_sem.at[t], left_recv.at[t], z + 1, y
        )

    def go_left(t):
        return remote(
            to_left.at[t], from_right.at[t], left_sem.at[t], right_recv.at[t], z - 1, y
        )

    chunk = 256
    for k in range(8):
        slot, t = k % 2, order[k // 2]
        if k + 1 < 8:
            load(k + 1)
        pltpu.make_async_copy(
            value_own.at[:, pl.ds(0, width)], loaded.at[slot], load_sem.at[slot]
        ).wait()

        @pl.loop(0, width // chunk)
        def _(c):
            cols = pl.ds(pl.multiple_of(c * chunk, chunk), chunk)
            product = dot(squared[...], loaded[slot, :, cols])
            if k % 2 == 0:
                across[t, :tokens, cols] = product.astype(jnp.bfloat16)
            else:
                total[t, :, cols] = product

        if k % 2 == 0:
            across[t, tokens:, :] = as_tail(row)
            go_across(t).start()

    def take(t, arrivals, recv):
        pltpu.make_async_copy(arrivals.at[t], arrivals.at[t], recv.at[t]).wait()
        total[t] += arrivals[t, :tokens, :].astype(jnp.float32)
        inner[t] += from_tail(arrivals[t, tokens:, :])

    def put(t, departures, copy):
        departures[t, :tokens, :] = total[t].astype(jnp.bfloat16)
        departures[t, tokens:, :] = as_tail(inner[t])
        copy.start()

    for t in order:
        inner[t] = row
        take(t, from_across, across_recv)
        pl.when((t >= z) & (z > 0))(lambda: take(t, from_left, left_recv))
        pl.when((t <= z) & (z < 3))(lambda: take(t, from_right, right_recv))
        pl.when(t > z)(lambda: put(t, to_right, go_right(t)))
        pl.when(t < z)(lambda: put(t, to_left, go_left(t)))

    amount = contract_first(as_tail(inner[z]), ones) * noise_scale
    for t in range(tokens // members):
        own = slice(t * members, (t + 1) * members)
        for c in range(0, width, 128):
            cols = slice(c, c + 128)
            spread = value_right[:, cols].astype(jnp.float32)
            out[own, cols] = (
                (total[z, own, cols] + amount[own, :] * spread) * inv_hidden
            ).astype(jnp.bfloat16)

    for t in order:
        go_across(t).wait_send()
        pl.when(t > z)(lambda: go_right(t).wait_send())
        pl.when(t < z)(lambda: go_left(t).wait_send())


def value_scatter(squared, inner_value, value_own, value_peer, value_right, inv_hidden):
    tokens = squared.shape[0]
    rows = value_own.shape[0]
    width = value_right.shape[1]
    vmem = pl.BlockSpec(memory_space=pltpu.VMEM)
    hbm = pl.BlockSpec(memory_space=pl.ANY)
    message = pltpu.VMEM((4, tokens + pad_rows, width), jnp.bfloat16)
    sems = pltpu.SemaphoreType.DMA((4,))
    return pl.pallas_call(
        functools.partial(value_scatter_kernel, inv_hidden),
        out_shape=jax.ShapeDtypeStruct((tokens, width), jnp.bfloat16),
        in_specs=[vmem, vmem, hbm, hbm, vmem],
        out_specs=vmem,
        scratch_shapes=[
            pltpu.VMEM((2, rows, width), jnp.bfloat16),
            pltpu.VMEM((4, tokens, width), jnp.float32),
            pltpu.VMEM((4, pad_rows, tokens), jnp.float32),
            message, message, message, message, message, message,
            pltpu.SemaphoreType.DMA((2,)),
            sems, sems, sems, sems, sems, sems,
        ],
        compiler_params=pltpu.CompilerParams(
            vmem_limit_bytes=vmem_bytes, collective_id=2, has_side_effects=True
        ),
        cost_estimate=pl.CostEstimate(
            flops=16 * tokens * width * rows,
            bytes_accessed=16 * width * rows,
            transcendentals=0,
        ),
        name="value_scatter",
    )(squared, inner_value, value_own, value_peer, value_right)


def key_step_kernel(step, side_ref, left_own, left_peer, right_own, right_peer, weight, out_ref):
    columns = out_ref.shape[1]
    chunk = min(512, columns)
    own, peer = left_own[0], left_peer[0]
    for c in range(0, columns, chunk):
        cols = slice(c, c + chunk)
        grad = contract_first(own, right_own[:, cols]) + contract_first(peer, right_peer[:, cols])
        out_ref[:, cols] = (weight[:, cols].astype(jnp.float32) + step * grad).astype(jnp.bfloat16)


def key_step(side, left_all, left_peer, right_own, right_peer, weight, step):
    half, members, width = left_peer.shape
    rows, columns = weight.shape
    fixed = pl.BlockSpec((members, columns), lambda j, s: (0, 0))
    tile = pl.BlockSpec((width, columns), lambda j, s: (j, 0))
    return pl.pallas_call(
        functools.partial(key_step_kernel, step),
        out_shape=jax.ShapeDtypeStruct(weight.shape, jnp.bfloat16),
        grid_spec=pltpu.PrefetchScalarGridSpec(
            num_scalar_prefetch=1,
            grid=(half,),
            in_specs=[
                pl.BlockSpec((1, members, width), lambda j, s: (s[0] * half + j, 0, 0)),
                pl.BlockSpec((1, members, width), lambda j, s: (j, 0, 0)),
                fixed,
                fixed,
                tile,
            ],
            out_specs=tile,
        ),
        compiler_params=pltpu.CompilerParams(vmem_limit_bytes=vmem_bytes),
        cost_estimate=pl.CostEstimate(
            flops=4 * members * rows * columns,
            bytes_accessed=4 * rows * columns + 4 * members * (rows + columns),
            transcendentals=0,
        ),
        name="key_step",
    )(side, left_all, left_peer, right_own, right_peer, weight)


def value_step_kernel(step, side_ref, left_own, left_peer, right_all, right_peer, weight, out_ref):
    half, _, width = right_peer.shape
    mine = side_ref[0] * half
    own, peer = left_own[...], left_peer[...]
    for j in range(half):
        cols = slice(j * width, (j + 1) * width)
        grad = contract_first(own, right_all[mine + j]) + contract_first(peer, right_peer[j])
        out_ref[:, cols] = (weight[:, cols].astype(jnp.float32) + step * grad).astype(jnp.bfloat16)


def value_step(side, left_own, left_peer, right_all, right_peer, weight, step):
    half, members, width = right_peer.shape
    rows, columns = weight.shape
    size = min(512, rows)
    side_tile = pl.BlockSpec((members, size), lambda i, s: (0, i))
    tile = pl.BlockSpec((size, columns), lambda i, s: (i, 0))
    return pl.pallas_call(
        functools.partial(value_step_kernel, step),
        out_shape=jax.ShapeDtypeStruct(weight.shape, jnp.bfloat16),
        grid_spec=pltpu.PrefetchScalarGridSpec(
            num_scalar_prefetch=1,
            grid=(rows // size,),
            in_specs=[
                side_tile,
                side_tile,
                pl.BlockSpec(right_all.shape, lambda i, s: (0, 0, 0)),
                pl.BlockSpec(right_peer.shape, lambda i, s: (0, 0, 0)),
                tile,
            ],
            out_specs=tile,
        ),
        compiler_params=pltpu.CompilerParams(vmem_limit_bytes=vmem_bytes),
        cost_estimate=pl.CostEstimate(
            flops=4 * members * rows * columns,
            bytes_accessed=4 * rows * columns + 4 * members * (rows + columns),
            transcendentals=0,
        ),
        name="value_step",
    )(side, left_own, left_peer, right_all, right_peer, weight)


def shards(
    token_ids, ranks, embedding, mix_key, key_weight, value_weight,
    key_left, key_right, value_left, value_right,
):
    members = ranks.shape[0]
    population = members * lax.axis_size("pop")
    side = lax.axis_index("pop")
    side_ref = side.astype(jnp.int32).reshape(1)
    slices = lax.axis_size("mp")
    half = slices // 2
    width = embedding.shape[1]
    model = slices * width
    hidden = slices * key_weight.shape[1]
    swap = lambda array: lax.ppermute(array, "pop", [(0, 1), (1, 0)])

    half_vocab = embedding.shape[0]
    by_side = jnp.swapaxes(token_ids.reshape(2, members, 2), 1, 2)

    def look(which):
        ids = lax.dynamic_index_in_dim(by_side, which, 0, keepdims=False).reshape(-1)
        ids = ids - side * half_vocab
        inside = (ids >= 0) & (ids < half_vocab)
        return jnp.take(embedding, jnp.clip(ids, 0, half_vocab - 1), axis=0, mode="clip"), inside

    theirs, _ = look(1 - side)
    received = swap(theirs)
    mine, inside = look(side)
    rows = jnp.where(inside[:, None], mine, received).astype(jnp.float32)
    first, second = rows[:members], rows[members:]
    keyed = jnp.concatenate(
        [first + (0.0 - first) * mix_key, second + (first - second) * mix_key], axis=0
    ).astype(jnp.bfloat16)
    left = key_left.astype(jnp.float32)
    inner = jnp.sum(
        keyed.astype(jnp.float32).reshape(2, members, width) * left[None], axis=2
    ).reshape(-1)
    groups = -(-2 * members // width)
    tail = jnp.stack(split(inner)).reshape(3 * groups, width)
    tail = jnp.pad(tail, ((0, pad_rows - 3 * groups), (0, 0)))
    keyed = jnp.concatenate([keyed, tail], axis=0)
    right_all = lax.all_gather(value_right, "mp", axis=0)
    left_all = lax.all_gather(key_left, "mp", axis=0)

    key_peer, value_peer = swap(key_weight), swap(value_weight)
    if slices == 8 and 2 * members == width:
        squared, inner_value = gather_key(
            keyed, key_weight, key_peer, key_right, value_left, model ** -0.5
        )
        mixed = value_scatter(
            squared, inner_value, value_weight, value_peer, value_right, hidden ** -0.5
        )
    else:
        partial = forward(
            side_ref, lax.all_gather(keyed, "mp", axis=0), key_weight, key_peer, value_weight,
            value_peer, key_right, value_left, right_all, model ** -0.5, hidden ** -0.5,
        )
        mixed = lax.psum_scatter(partial, "mp", scatter_dimension=0, tiled=False)
    mixed = jnp.swapaxes(mixed.reshape(2, members, width), 0, 1).reshape(2 * members, width)

    fitness = (2 * ranks - (population - 1)).astype(jnp.float32) / (population - 1)
    scaled_right = (fitness[:, None] * key_right.astype(jnp.float32)).astype(jnp.bfloat16)
    scaled_left = (fitness[:, None] * value_left.astype(jnp.float32)).astype(jnp.bfloat16)
    other = (1 - side) * half
    left_peer = swap(lax.dynamic_slice_in_dim(left_all, other, half, 0))
    right_peer = swap(lax.dynamic_slice_in_dim(right_all, other, half, 0))
    step = step_scale / population
    new_key = key_step(
        side_ref, left_all, left_peer, scaled_right, swap(scaled_right), key_weight, step
    )
    new_value = value_step(
        side_ref, scaled_left, swap(scaled_left), right_all, right_peer, value_weight, step
    )
    return (mixed, new_key, new_value)


def solution(mesh):
    placed = (
        P("grp", None),
        P(("grp", "pop")),
        P("pop", "mp"),
        P("mp"),
        P("pop", "mp"),
        P("mp", "pop"),
        P(("grp", "pop"), "mp"),
        P(("grp", "pop"), "mp"),
        P(("grp", "pop"), "mp"),
        P(("grp", "pop"), "mp"),
    )
    return jax.shard_map(
        shards,
        mesh=mesh,
        in_specs=placed,
        out_specs=(P(("grp", "pop"), "mp"), P(("grp", "pop"), "mp"), P(("grp", "mp"), "pop")),
        check_vma=False,
    )
```

```python
import functools

import jax
import jax.numpy as jnp
from jax import lax
from jax.experimental import pallas as pl
from jax.experimental.pallas import tpu as pltpu
from jax.sharding import PartitionSpec as P

noise_scale = 0.5
step_scale = 8.0
vmem_bytes = 58 * 1024 * 1024
pad_rows = 16


def dot(left, right):
    return jnp.dot(left, right, preferred_element_type=jnp.float32)


def contract_first(left, right):
    return lax.dot_general(
        left, right, (((0,), (0,)), ((), ())), preferred_element_type=jnp.float32
    )


def forward_kernel(
    inv_model, inv_hidden, side_ref, keyed_ref, key_own, key_peer, value_own, value_peer,
    key_right, value_left, value_right, out_ref, total, inner_key, inner_value,
):
    step, last = pl.program_id(0), pl.num_programs(0) - 1
    slices, padded, width = keyed_ref.shape
    tokens, half = padded - pad_rows, slices // 2
    tile = key_own.shape[1]
    mine = side_ref[0] * half
    theirs = half - mine

    @pl.when(step == 0)
    def _():
        groups = tokens // width
        line = lax.broadcasted_iota(jnp.int32, (pad_rows, 128), 0)
        for g in range(groups):
            chosen = (line < 3 * groups) & (line % groups == g)
            ones = jnp.where(chosen, 1.0, 0.0).astype(jnp.bfloat16)
            partial = jnp.zeros((width, 128), jnp.float32)
            for s in range(slices):
                partial += contract_first(keyed_ref[s, tokens:, :], ones)
            inner_key[g * width : (g + 1) * width, :] = partial * (noise_scale * inv_model)
        inner_value[...] = jnp.zeros_like(inner_value)

    projected = jnp.zeros((tokens, tile), jnp.float32)
    for j in range(half):
        rows = slice(j * width, (j + 1) * width)
        projected += dot(keyed_ref[mine + j, :tokens, :], key_own[rows, :])
        projected += dot(keyed_ref[theirs + j, :tokens, :], key_peer[rows, :])
    right = key_right[...].astype(jnp.float32)
    left = value_left[...].astype(jnp.float32)
    members = right.shape[0]
    parts = []
    for t in range(tokens // members):
        own = slice(t * members, (t + 1) * members)
        pieces = []
        for c in range(0, tile, 128):
            cols = slice(c, c + 128)
            hidden = projected[own, cols] * inv_model + inner_key[own, :] * right[:, cols]
            rounded = (jnp.maximum(hidden, 0.0) ** 2).astype(jnp.bfloat16)
            inner_value[own, :] += rounded.astype(jnp.float32) * left[:, cols]
            pieces.append(rounded)
        parts.append(jnp.concatenate(pieces, axis=1))
    squared = jnp.concatenate(parts, axis=0)

    for j in range(half):
        cols = slice(j * width, (j + 1) * width)
        for base, weight in ((mine, value_own), (theirs, value_peer)):
            product = dot(squared, weight[:, cols])

            @pl.when(step == 0)
            def _():
                total[base + j] = product

            @pl.when(step > 0)
            def _():
                total[base + j] += product

    @pl.when(step == last)
    def _():
        amount = noise_scale * jnp.sum(inner_value[...], axis=1, keepdims=True)
        for s in range(slices):
            spread = value_right[s].astype(jnp.float32)
            for t in range(tokens // members):
                own = slice(t * members, (t + 1) * members)
                out_ref[s, own, :] = (
                    (total[s, own, :] + amount[own, :] * spread) * inv_hidden
                ).astype(jnp.bfloat16)


def forward(side, keyed, key_own, key_peer, value_own, value_peer, key_right, value_left,
            value_right, inv_model, inv_hidden):
    slices, padded, width = keyed.shape
    tokens = padded - pad_rows
    rows, hidden = key_own.shape
    members = key_right.shape[0]
    tile = min(512, hidden)
    whole = lambda i, s: (0, 0, 0)
    column = lambda i, s: (0, i)
    row = lambda i, s: (i, 0)
    return pl.pallas_call(
        functools.partial(forward_kernel, inv_model, inv_hidden),
        out_shape=jax.ShapeDtypeStruct((slices, tokens, width), jnp.bfloat16),
        grid_spec=pltpu.PrefetchScalarGridSpec(
            num_scalar_prefetch=1,
            grid=(hidden // tile,),
            in_specs=[
                pl.BlockSpec(keyed.shape, whole),
                pl.BlockSpec((rows, tile), column),
                pl.BlockSpec((rows, tile), column),
                pl.BlockSpec((tile, rows), row),
                pl.BlockSpec((tile, rows), row),
                pl.BlockSpec((members, tile), column),
                pl.BlockSpec((members, tile), column),
                pl.BlockSpec(value_right.shape, whole),
            ],
            out_specs=pl.BlockSpec((slices, tokens, width), whole),
            scratch_shapes=[
                pltpu.VMEM((slices, tokens, width), jnp.float32),
                pltpu.VMEM((tokens, 128), jnp.float32),
                pltpu.VMEM((tokens, 128), jnp.float32),
            ],
        ),
        compiler_params=pltpu.CompilerParams(vmem_limit_bytes=vmem_bytes),
        cost_estimate=pl.CostEstimate(
            flops=8 * tokens * rows * hidden,
            bytes_accessed=8 * rows * hidden + 4 * tokens * slices * width,
            transcendentals=0,
        ),
        name="forward",
    )(side, keyed, key_own, key_peer, value_own, value_peer, key_right, value_left, value_right)


def coordinates():
    place = lax.axis_index("mp")
    return lax.div(place, 2), lax.rem(place, 2)


def pick(z, table):
    total = 0
    for value, row in enumerate(table):
        total = total + (1 - lax.div(lax.rem(z + 4 - value, 4) + 3, 4)) * row
    return total


def greet(z, y):
    barrier = pltpu.get_barrier_semaphore()

    def tell(zz, yy):
        pl.semaphore_signal(
            barrier, inc=1, device_id={"mp": 2 * zz + yy}, device_id_type=pl.DeviceIdType.MESH
        )

    tell(z, 1 - y)
    pl.when(z > 0)(lambda: tell(z - 1, y))
    pl.when(z < 3)(lambda: tell(z + 1, y))
    pl.semaphore_wait(barrier, 1 + lax.div(z + 3, 4) + lax.div(6 - z, 4))


def remote(source, target, send, recv, zz, yy):
    return pltpu.make_async_remote_copy(
        src_ref=source,
        dst_ref=target,
        send_sem=send,
        recv_sem=recv,
        device_id={"mp": 2 * zz + yy},
        device_id_type=pl.DeviceIdType.MESH,
    )


def split(row):
    high = row.astype(jnp.bfloat16)
    rest = row - high.astype(jnp.float32)
    middle = rest.astype(jnp.bfloat16)
    low = (rest - middle.astype(jnp.float32)).astype(jnp.bfloat16)
    return high, middle, low


def as_tail(row):
    line = lax.broadcasted_iota(jnp.int32, row.shape, 0)
    high, middle, low = [term.astype(jnp.float32) for term in split(row)]
    kept = jnp.where(line == 0, high, jnp.where(line == 1, middle, jnp.where(line == 2, low, 0.0)))
    return kept.astype(jnp.bfloat16)


def from_tail(tail):
    total = jnp.sum(tail.astype(jnp.float32), axis=0, keepdims=True)
    return jnp.broadcast_to(total, tail.shape)


gather_order = ((0, 1, 2, 3), (1, 0, 2, 3), (2, 3, 1, 0), (3, 2, 1, 0))
scatter_order = ((3, 2, 1, 0), (3, 0, 2, 1), (0, 3, 1, 2), (0, 1, 2, 3))


def gather_key_kernel(
    inv_model, keyed, key_own, key_peer, key_right, value_left, squared, inner_value,
    held, loaded, projected, inner_key, load_sem, right_sem, left_sem, across_sem, recv_sem,
):
    z, y = coordinates()
    side = lax.axis_index("pop")
    slices, padded, width = held.shape
    tokens, half = padded - pad_rows, slices // 2
    hidden = key_own.shape[1]
    members = key_right.shape[0]
    order = [pick(z, [row[k] for row in gather_order]) for k in range(4)]
    own = [2 * b + y for b in order]
    other = [2 * b + 1 - y for b in order]
    sequence = [own[0], own[1], other[0], own[2], other[1], own[3], other[2], other[3]]

    def load(k):
        block, slot = sequence[k], k % 2
        row = pl.multiple_of(lax.rem(block, half) * width, width)
        from_own = lax.div(block, half) == side

        @pl.when(from_own)
        def _():
            pltpu.make_async_copy(
                key_own.at[pl.ds(row, width), :], loaded.at[slot], load_sem.at[slot]
            ).start()

        @pl.when(jnp.logical_not(from_own))
        def _():
            pltpu.make_async_copy(
                key_peer.at[pl.ds(row, width), :], loaded.at[slot], load_sem.at[slot]
            ).start()

    load(0)
    held[own[0]] = keyed[...]
    greet(z, y)

    def go_right(b):
        block = held.at[2 * b + y]
        return remote(block, block, right_sem.at[b], recv_sem.at[2 * b + y], z + 1, y)

    def go_left(b):
        block = held.at[2 * b + y]
        return remote(block, block, left_sem.at[b], recv_sem.at[2 * b + y], z - 1, y)

    def go_across(b):
        block = held.at[2 * b + y]
        return remote(block, block, across_sem.at[b], recv_sem.at[2 * b + y], z, 1 - y)

    def arrived(block):
        pltpu.make_async_copy(held.at[block], held.at[block], recv_sem.at[block]).wait()

    def forward_on(k, act):
        b = order[k]
        pl.when((b <= z) & (z < 3))(lambda: act(go_right(b)))
        pl.when((b >= z) & (z > 0))(lambda: act(go_left(b)))
        act(go_across(b))

    ones = jnp.ones((pad_rows, 128), jnp.bfloat16)
    chunk = 512

    def compute(k):
        block, slot = sequence[k], k % 2
        if k + 1 < len(sequence):
            load(k + 1)
        pltpu.make_async_copy(
            key_own.at[pl.ds(0, width), :], loaded.at[slot], load_sem.at[slot]
        ).wait()
        partial = contract_first(held[block, tokens:, :], ones)
        inner_key[...] = partial if k == 0 else inner_key[...] + partial

        @pl.loop(0, hidden // chunk)
        def _(c):
            cols = pl.ds(pl.multiple_of(c * chunk, chunk), chunk)
            product = dot(held[block, :tokens, :], loaded[slot, :, cols])
            projected[:, cols] = product if k == 0 else projected[:, cols] + product

    k = 0
    for step in range(4):
        if step > 0:
            arrived(own[step])
        forward_on(step, lambda copy: copy.start())
        compute(k)
        k += 1
        if step > 0:
            arrived(other[step - 1])
            compute(k)
            k += 1
    arrived(other[3])
    compute(k)

    factor = inner_key[...] * (noise_scale * inv_model)
    inner_key[...] = factor
    inner_value[...] = jnp.zeros_like(inner_value)

    @pl.loop(0, hidden // 128)
    def _(c):
        cols = pl.ds(pl.multiple_of(c * 128, 128), 128)
        right = key_right[:, cols].astype(jnp.float32)
        left = value_left[:, cols].astype(jnp.float32)
        for t in range(tokens // members):
            rows = slice(t * members, (t + 1) * members)
            value = projected[rows, cols] * inv_model + inner_key[rows, :] * right
            rounded = (jnp.maximum(value, 0.0) ** 2).astype(jnp.bfloat16)
            squared[rows, cols] = rounded
            inner_value[rows, :] += rounded.astype(jnp.float32) * left

    for step in range(4):
        forward_on(step, lambda copy: copy.wait_send())


def gather_key(keyed, key_own, key_peer, key_right, value_left, inv_model):
    padded, width = keyed.shape
    tokens = padded - pad_rows
    hidden = key_own.shape[1]
    slices = 8
    vmem = pl.BlockSpec(memory_space=pltpu.VMEM)
    hbm = pl.BlockSpec(memory_space=pl.ANY)
    return pl.pallas_call(
        functools.partial(gather_key_kernel, inv_model),
        out_shape=(
            jax.ShapeDtypeStruct((tokens, hidden), jnp.bfloat16),
            jax.ShapeDtypeStruct((tokens, 128), jnp.float32),
        ),
        in_specs=[vmem, hbm, hbm, vmem, vmem],
        out_specs=(vmem, vmem),
        scratch_shapes=[
            pltpu.VMEM((slices, padded, width), jnp.bfloat16),
            pltpu.VMEM((2, width, hidden), jnp.bfloat16),
            pltpu.VMEM((tokens, hidden), jnp.float32),
            pltpu.VMEM((tokens, 128), jnp.float32),
            pltpu.SemaphoreType.DMA((2,)),
            pltpu.SemaphoreType.DMA((4,)),
            pltpu.SemaphoreType.DMA((4,)),
            pltpu.SemaphoreType.DMA((4,)),
            pltpu.SemaphoreType.DMA((slices,)),
        ],
        compiler_params=pltpu.CompilerParams(
            vmem_limit_bytes=vmem_bytes, collective_id=1, has_side_effects=True
        ),
        cost_estimate=pl.CostEstimate(
            flops=16 * tokens * width * hidden,
            bytes_accessed=16 * width * hidden,
            transcendentals=0,
        ),
        name="gather_key",
    )(keyed, key_own, key_peer, key_right, value_left)


def value_scatter_kernel(
    inv_hidden, squared, inner_value, value_own, value_peer, value_right, out,
    loaded, total, inner, across, from_across, to_right, to_left, from_left, from_right,
    load_sem, across_sem, across_recv, right_sem, left_sem, left_recv, right_recv,
):
    z, y = coordinates()
    side = lax.axis_index("pop")
    rows, width = loaded.shape[1], loaded.shape[2]
    tokens = squared.shape[0]
    members = value_right.shape[0]
    half = 4
    order = [pick(z, [row[k] for row in scatter_order]) for k in range(4)]
    sequence = []
    for t in order:
        sequence += [2 * t + 1 - y, 2 * t + y]

    def load(k):
        block, slot = sequence[k], k % 2
        column = pl.multiple_of(lax.rem(block, half) * width, width)
        from_own = lax.div(block, half) == side

        @pl.when(from_own)
        def _():
            pltpu.make_async_copy(
                value_own.at[:, pl.ds(column, width)], loaded.at[slot], load_sem.at[slot]
            ).start()

        @pl.when(jnp.logical_not(from_own))
        def _():
            pltpu.make_async_copy(
                value_peer.at[:, pl.ds(column, width)], loaded.at[slot], load_sem.at[slot]
            ).start()

    load(0)
    greet(z, y)
    ones = jnp.ones((pad_rows, 128), jnp.bfloat16)
    row = jnp.zeros((pad_rows, tokens), jnp.float32)
    for term in split(inner_value[...]):
        row += lax.dot_general(
            ones, term, (((1,), (1,)), ((), ())), preferred_element_type=jnp.float32
        )

    def go_across(t):
        return remote(
            across.at[t], from_across.at[t], across_sem.at[t], across_recv.at[t], z, 1 - y
        )

    def go_right(t):
        return remote(
            to_right.at[t], from_left.at[t], right_sem.at[t], left_recv.at[t], z + 1, y
        )

    def go_left(t):
        return remote(
            to_left.at[t], from_right.at[t], left_sem.at[t], right_recv.at[t], z - 1, y
        )

    chunk = 256
    for k in range(8):
        slot, t = k % 2, order[k // 2]
        if k + 1 < 8:
            load(k + 1)
        pltpu.make_async_copy(
            value_own.at[:, pl.ds(0, width)], loaded.at[slot], load_sem.at[slot]
        ).wait()

        @pl.loop(0, width // chunk)
        def _(c):
            cols = pl.ds(pl.multiple_of(c * chunk, chunk), chunk)
            product = dot(squared[...], loaded[slot, :, cols])
            if k % 2 == 0:
                across[t, :tokens, cols] = product.astype(jnp.bfloat16)
            else:
                total[t, :, cols] = product

        if k % 2 == 0:
            across[t, tokens:, :] = as_tail(row)
            go_across(t).start()

    def take(t, arrivals, recv):
        pltpu.make_async_copy(arrivals.at[t], arrivals.at[t], recv.at[t]).wait()
        total[t] += arrivals[t, :tokens, :].astype(jnp.float32)
        inner[t] += from_tail(arrivals[t, tokens:, :])

    def put(t, departures, copy):
        departures[t, :tokens, :] = total[t].astype(jnp.bfloat16)
        departures[t, tokens:, :] = as_tail(inner[t])
        copy.start()

    for t in order:
        inner[t] = row
        take(t, from_across, across_recv)
        pl.when((t >= z) & (z > 0))(lambda: take(t, from_left, left_recv))
        pl.when((t <= z) & (z < 3))(lambda: take(t, from_right, right_recv))
        pl.when(t > z)(lambda: put(t, to_right, go_right(t)))
        pl.when(t < z)(lambda: put(t, to_left, go_left(t)))

    amount = contract_first(as_tail(inner[z]), ones) * noise_scale
    for t in range(tokens // members):
        own = slice(t * members, (t + 1) * members)
        for c in range(0, width, 128):
            cols = slice(c, c + 128)
            spread = value_right[:, cols].astype(jnp.float32)
            out[own, cols] = (
                (total[z, own, cols] + amount[own, :] * spread) * inv_hidden
            ).astype(jnp.bfloat16)

    for t in order:
        go_across(t).wait_send()
        pl.when(t > z)(lambda: go_right(t).wait_send())
        pl.when(t < z)(lambda: go_left(t).wait_send())


def value_scatter(squared, inner_value, value_own, value_peer, value_right, inv_hidden):
    tokens = squared.shape[0]
    rows = value_own.shape[0]
    width = value_right.shape[1]
    vmem = pl.BlockSpec(memory_space=pltpu.VMEM)
    hbm = pl.BlockSpec(memory_space=pl.ANY)
    message = pltpu.VMEM((4, tokens + pad_rows, width), jnp.bfloat16)
    sems = pltpu.SemaphoreType.DMA((4,))
    return pl.pallas_call(
        functools.partial(value_scatter_kernel, inv_hidden),
        out_shape=jax.ShapeDtypeStruct((tokens, width), jnp.bfloat16),
        in_specs=[vmem, vmem, hbm, hbm, vmem],
        out_specs=vmem,
        scratch_shapes=[
            pltpu.VMEM((2, rows, width), jnp.bfloat16),
            pltpu.VMEM((4, tokens, width), jnp.float32),
            pltpu.VMEM((4, pad_rows, tokens), jnp.float32),
            message, message, message, message, message, message,
            pltpu.SemaphoreType.DMA((2,)),
            sems, sems, sems, sems, sems, sems,
        ],
        compiler_params=pltpu.CompilerParams(
            vmem_limit_bytes=vmem_bytes, collective_id=2, has_side_effects=True
        ),
        cost_estimate=pl.CostEstimate(
            flops=16 * tokens * width * rows,
            bytes_accessed=16 * width * rows,
            transcendentals=0,
        ),
        name="value_scatter",
    )(squared, inner_value, value_own, value_peer, value_right)


def key_step_kernel(
    step, side_ref, left_own, left_peer, right_own, right_peer, weight, after, out_ref
):
    columns = out_ref.shape[1]
    chunk = min(512, columns)
    own, peer = left_own[0], left_peer[0]
    for c in range(0, columns, chunk):
        cols = slice(c, c + chunk)
        grad = contract_first(own, right_own[:, cols]) + contract_first(peer, right_peer[:, cols])
        out_ref[:, cols] = (weight[:, cols].astype(jnp.float32) + step * grad).astype(jnp.bfloat16)


def key_step(side, left_all, left_peer, right_own, right_peer, weight, step, after):
    half, members, width = left_peer.shape
    rows, columns = weight.shape
    fixed = pl.BlockSpec((members, columns), lambda j, s: (0, 0))
    tile = pl.BlockSpec((width, columns), lambda j, s: (j, 0))
    return pl.pallas_call(
        functools.partial(key_step_kernel, step),
        out_shape=jax.ShapeDtypeStruct(weight.shape, jnp.bfloat16),
        grid_spec=pltpu.PrefetchScalarGridSpec(
            num_scalar_prefetch=1,
            grid=(half,),
            in_specs=[
                pl.BlockSpec((1, members, width), lambda j, s: (s[0] * half + j, 0, 0)),
                pl.BlockSpec((1, members, width), lambda j, s: (j, 0, 0)),
                fixed,
                fixed,
                tile,
                pl.BlockSpec(memory_space=pl.ANY),
            ],
            out_specs=tile,
        ),
        compiler_params=pltpu.CompilerParams(vmem_limit_bytes=vmem_bytes),
        cost_estimate=pl.CostEstimate(
            flops=4 * members * rows * columns,
            bytes_accessed=4 * rows * columns + 4 * members * (rows + columns),
            transcendentals=0,
        ),
        name="key_step",
    )(side, left_all, left_peer, right_own, right_peer, weight, after)


def value_step_kernel(
    step, side_ref, left_own, left_peer, right_all, right_peer, weight, after, out_ref
):
    half, _, width = right_peer.shape
    mine = side_ref[0] * half
    own, peer = left_own[...], left_peer[...]
    for j in range(half):
        cols = slice(j * width, (j + 1) * width)
        grad = contract_first(own, right_all[mine + j]) + contract_first(peer, right_peer[j])
        out_ref[:, cols] = (weight[:, cols].astype(jnp.float32) + step * grad).astype(jnp.bfloat16)


def value_step(side, left_own, left_peer, right_all, right_peer, weight, step, after):
    half, members, width = right_peer.shape
    rows, columns = weight.shape
    size = min(512, rows)
    side_tile = pl.BlockSpec((members, size), lambda i, s: (0, i))
    tile = pl.BlockSpec((size, columns), lambda i, s: (i, 0))
    return pl.pallas_call(
        functools.partial(value_step_kernel, step),
        out_shape=jax.ShapeDtypeStruct(weight.shape, jnp.bfloat16),
        grid_spec=pltpu.PrefetchScalarGridSpec(
            num_scalar_prefetch=1,
            grid=(rows // size,),
            in_specs=[
                side_tile,
                side_tile,
                pl.BlockSpec(right_all.shape, lambda i, s: (0, 0, 0)),
                pl.BlockSpec(right_peer.shape, lambda i, s: (0, 0, 0)),
                tile,
                pl.BlockSpec(memory_space=pl.ANY),
            ],
            out_specs=tile,
        ),
        compiler_params=pltpu.CompilerParams(vmem_limit_bytes=vmem_bytes),
        cost_estimate=pl.CostEstimate(
            flops=4 * members * rows * columns,
            bytes_accessed=4 * rows * columns + 4 * members * (rows + columns),
            transcendentals=0,
        ),
        name="value_step",
    )(side, left_own, left_peer, right_all, right_peer, weight, after)


def shards(
    token_ids, ranks, embedding, mix_key, key_weight, value_weight,
    key_left, key_right, value_left, value_right,
):
    members = ranks.shape[0]
    population = members * lax.axis_size("pop")
    side = lax.axis_index("pop")
    side_ref = side.astype(jnp.int32).reshape(1)
    slices = lax.axis_size("mp")
    half = slices // 2
    width = embedding.shape[1]
    model = slices * width
    hidden = slices * key_weight.shape[1]
    swap = lambda array: lax.ppermute(array, "pop", [(0, 1), (1, 0)])

    half_vocab = embedding.shape[0]
    by_side = jnp.swapaxes(token_ids.reshape(2, members, 2), 1, 2)

    tokens = 2 * members
    ids = jnp.concatenate(
        [
            lax.dynamic_index_in_dim(by_side, side, 0, keepdims=False).reshape(-1),
            lax.dynamic_index_in_dim(by_side, 1 - side, 0, keepdims=False).reshape(-1),
        ]
    )
    ids = ids - side * half_vocab
    inside = (ids[:tokens] >= 0) & (ids[:tokens] < half_vocab)
    looked = jnp.take(embedding, jnp.clip(ids, 0, half_vocab - 1), axis=0, mode="clip")
    received = swap(looked[tokens:])
    rows = jnp.where(inside[:, None], looked[:tokens], received).astype(jnp.float32)
    first, second = rows[:members], rows[members:]
    keyed = jnp.concatenate(
        [first + (0.0 - first) * mix_key, second + (first - second) * mix_key], axis=0
    ).astype(jnp.bfloat16)
    left = key_left.astype(jnp.float32)
    inner = jnp.sum(
        keyed.astype(jnp.float32).reshape(2, members, width) * left[None], axis=2
    ).reshape(-1)
    groups = -(-2 * members // width)
    tail = jnp.stack(split(inner)).reshape(3 * groups, width)
    tail = jnp.pad(tail, ((0, pad_rows - 3 * groups), (0, 0)))
    keyed = jnp.concatenate([keyed, tail], axis=0)
    right_all = lax.all_gather(value_right, "mp", axis=0)
    left_all = lax.all_gather(key_left, "mp", axis=0)

    key_peer, value_peer = swap(key_weight), swap(value_weight)
    if slices == 8 and 2 * members == width:
        squared, inner_value = gather_key(
            keyed, key_weight, key_peer, key_right, value_left, model ** -0.5
        )
        right_all, squared = lax.optimization_barrier((right_all, squared))
        mixed = value_scatter(
            squared, inner_value, value_weight, value_peer, value_right, hidden ** -0.5
        )
        left_all, mixed = lax.optimization_barrier((left_all, mixed))
    else:
        partial = forward(
            side_ref, lax.all_gather(keyed, "mp", axis=0), key_weight, key_peer, value_weight,
            value_peer, key_right, value_left, right_all, model ** -0.5, hidden ** -0.5,
        )
        mixed = lax.psum_scatter(partial, "mp", scatter_dimension=0, tiled=False)
    summed = mixed
    mixed = jnp.swapaxes(mixed.reshape(2, members, width), 0, 1).reshape(2 * members, width)

    fitness = (2 * ranks - (population - 1)).astype(jnp.float32) / (population - 1)
    scaled_right = (fitness[:, None] * key_right.astype(jnp.float32)).astype(jnp.bfloat16)
    scaled_left = (fitness[:, None] * value_left.astype(jnp.float32)).astype(jnp.bfloat16)
    other = (1 - side) * half
    left_peer = swap(lax.dynamic_slice_in_dim(left_all, other, half, 0))
    right_peer = swap(lax.dynamic_slice_in_dim(right_all, other, half, 0))
    step = step_scale / population
    new_key = key_step(
        side_ref, left_all, left_peer, scaled_right, swap(scaled_right), key_weight, step,
        summed,
    )
    new_value = value_step(
        side_ref, scaled_left, swap(scaled_left), right_all, right_peer, value_weight, step,
        summed,
    )
    return (mixed, new_key, new_value)


def solution(mesh):
    placed = (
        P("grp", None),
        P(("grp", "pop")),
        P("pop", "mp"),
        P("mp"),
        P("pop", "mp"),
        P("mp", "pop"),
        P(("grp", "pop"), "mp"),
        P(("grp", "pop"), "mp"),
        P(("grp", "pop"), "mp"),
        P(("grp", "pop"), "mp"),
    )
    return jax.shard_map(
        shards,
        mesh=mesh,
        in_specs=placed,
        out_specs=(P(("grp", "pop"), "mp"), P(("grp", "pop"), "mp"), P(("grp", "mp"), "pop")),
        check_vma=False,
    )
```

```python
import functools

import jax
import jax.numpy as jnp
from jax import lax
from jax.experimental import pallas as pl
from jax.experimental.pallas import tpu as pltpu
from jax.sharding import PartitionSpec as P

noise_scale = 0.5
step_scale = 8.0
vmem_bytes = 58 * 1024 * 1024
pad_rows = 16


def dot(left, right):
    return jnp.dot(left, right, preferred_element_type=jnp.float32)


def contract_first(left, right):
    return lax.dot_general(
        left, right, (((0,), (0,)), ((), ())), preferred_element_type=jnp.float32
    )


def forward_kernel(
    inv_model, inv_hidden, side_ref, keyed_ref, key_own, key_peer, value_own, value_peer,
    key_right, value_left, value_right, out_ref, total, inner_key, inner_value,
):
    step, last = pl.program_id(0), pl.num_programs(0) - 1
    slices, padded, width = keyed_ref.shape
    tokens, half = padded - pad_rows, slices // 2
    tile = key_own.shape[1]
    mine = side_ref[0] * half
    theirs = half - mine

    @pl.when(step == 0)
    def _():
        groups = tokens // width
        line = lax.broadcasted_iota(jnp.int32, (pad_rows, 128), 0)
        for g in range(groups):
            chosen = (line < 3 * groups) & (line % groups == g)
            ones = jnp.where(chosen, 1.0, 0.0).astype(jnp.bfloat16)
            partial = jnp.zeros((width, 128), jnp.float32)
            for s in range(slices):
                partial += contract_first(keyed_ref[s, tokens:, :], ones)
            inner_key[g * width : (g + 1) * width, :] = partial * (noise_scale * inv_model)
        inner_value[...] = jnp.zeros_like(inner_value)

    projected = jnp.zeros((tokens, tile), jnp.float32)
    for j in range(half):
        rows = slice(j * width, (j + 1) * width)
        projected += dot(keyed_ref[mine + j, :tokens, :], key_own[rows, :])
        projected += dot(keyed_ref[theirs + j, :tokens, :], key_peer[rows, :])
    right = key_right[...].astype(jnp.float32)
    left = value_left[...].astype(jnp.float32)
    members = right.shape[0]
    parts = []
    for t in range(tokens // members):
        own = slice(t * members, (t + 1) * members)
        pieces = []
        for c in range(0, tile, 128):
            cols = slice(c, c + 128)
            hidden = projected[own, cols] * inv_model + inner_key[own, :] * right[:, cols]
            rounded = (jnp.maximum(hidden, 0.0) ** 2).astype(jnp.bfloat16)
            inner_value[own, :] += rounded.astype(jnp.float32) * left[:, cols]
            pieces.append(rounded)
        parts.append(jnp.concatenate(pieces, axis=1))
    squared = jnp.concatenate(parts, axis=0)

    for j in range(half):
        cols = slice(j * width, (j + 1) * width)
        for base, weight in ((mine, value_own), (theirs, value_peer)):
            product = dot(squared, weight[:, cols])

            @pl.when(step == 0)
            def _():
                total[base + j] = product

            @pl.when(step > 0)
            def _():
                total[base + j] += product

    @pl.when(step == last)
    def _():
        amount = noise_scale * jnp.sum(inner_value[...], axis=1, keepdims=True)
        for s in range(slices):
            spread = value_right[s].astype(jnp.float32)
            for t in range(tokens // members):
                own = slice(t * members, (t + 1) * members)
                out_ref[s, own, :] = (
                    (total[s, own, :] + amount[own, :] * spread) * inv_hidden
                ).astype(jnp.bfloat16)


def forward(side, keyed, key_own, key_peer, value_own, value_peer, key_right, value_left,
            value_right, inv_model, inv_hidden):
    slices, padded, width = keyed.shape
    tokens = padded - pad_rows
    rows, hidden = key_own.shape
    members = key_right.shape[0]
    tile = min(512, hidden)
    whole = lambda i, s: (0, 0, 0)
    column = lambda i, s: (0, i)
    row = lambda i, s: (i, 0)
    return pl.pallas_call(
        functools.partial(forward_kernel, inv_model, inv_hidden),
        out_shape=jax.ShapeDtypeStruct((slices, tokens, width), jnp.bfloat16),
        grid_spec=pltpu.PrefetchScalarGridSpec(
            num_scalar_prefetch=1,
            grid=(hidden // tile,),
            in_specs=[
                pl.BlockSpec(keyed.shape, whole),
                pl.BlockSpec((rows, tile), column),
                pl.BlockSpec((rows, tile), column),
                pl.BlockSpec((tile, rows), row),
                pl.BlockSpec((tile, rows), row),
                pl.BlockSpec((members, tile), column),
                pl.BlockSpec((members, tile), column),
                pl.BlockSpec(value_right.shape, whole),
            ],
            out_specs=pl.BlockSpec((slices, tokens, width), whole),
            scratch_shapes=[
                pltpu.VMEM((slices, tokens, width), jnp.float32),
                pltpu.VMEM((tokens, 128), jnp.float32),
                pltpu.VMEM((tokens, 128), jnp.float32),
            ],
        ),
        compiler_params=pltpu.CompilerParams(vmem_limit_bytes=vmem_bytes),
        cost_estimate=pl.CostEstimate(
            flops=8 * tokens * rows * hidden,
            bytes_accessed=8 * rows * hidden + 4 * tokens * slices * width,
            transcendentals=0,
        ),
        name="forward",
    )(side, keyed, key_own, key_peer, value_own, value_peer, key_right, value_left, value_right)


def coordinates():
    place = lax.axis_index("mp")
    return lax.div(place, 2), lax.rem(place, 2)


def pick(z, table):
    total = 0
    for value, row in enumerate(table):
        total = total + (1 - lax.div(lax.rem(z + 4 - value, 4) + 3, 4)) * row
    return total


def greet(z, y):
    barrier = pltpu.get_barrier_semaphore()

    def tell(zz, yy):
        pl.semaphore_signal(
            barrier, inc=1, device_id={"mp": 2 * zz + yy}, device_id_type=pl.DeviceIdType.MESH
        )

    tell(z, 1 - y)
    pl.when(z > 0)(lambda: tell(z - 1, y))
    pl.when(z < 3)(lambda: tell(z + 1, y))
    pl.semaphore_wait(barrier, 1 + lax.div(z + 3, 4) + lax.div(6 - z, 4))


def remote(source, target, send, recv, zz, yy):
    return pltpu.make_async_remote_copy(
        src_ref=source,
        dst_ref=target,
        send_sem=send,
        recv_sem=recv,
        device_id={"mp": 2 * zz + yy},
        device_id_type=pl.DeviceIdType.MESH,
    )


def split(row):
    high = row.astype(jnp.bfloat16)
    rest = row - high.astype(jnp.float32)
    middle = rest.astype(jnp.bfloat16)
    low = (rest - middle.astype(jnp.float32)).astype(jnp.bfloat16)
    return high, middle, low


def as_tail(row):
    line = lax.broadcasted_iota(jnp.int32, row.shape, 0)
    high, middle, low = [term.astype(jnp.float32) for term in split(row)]
    kept = jnp.where(line == 0, high, jnp.where(line == 1, middle, jnp.where(line == 2, low, 0.0)))
    return kept.astype(jnp.bfloat16)


def from_tail(tail):
    total = jnp.sum(tail.astype(jnp.float32), axis=0, keepdims=True)
    return jnp.broadcast_to(total, tail.shape)


gather_order = ((0, 1, 2, 3), (1, 0, 2, 3), (2, 3, 1, 0), (3, 2, 1, 0))
scatter_order = ((3, 2, 1, 0), (3, 0, 2, 1), (0, 3, 1, 2), (0, 1, 2, 3))


def gather_key_kernel(
    inv_model, keyed, key_own, key_peer, key_right, value_left, squared, inner_value,
    held, loaded, projected, inner_key, load_sem, right_sem, left_sem, across_sem, recv_sem,
):
    z, y = coordinates()
    side = lax.axis_index("pop")
    slices, padded, width = held.shape
    tokens, half = padded - pad_rows, slices // 2
    hidden = key_own.shape[1]
    members = key_right.shape[0]
    order = [pick(z, [row[k] for row in gather_order]) for k in range(4)]
    own = [2 * b + y for b in order]
    other = [2 * b + 1 - y for b in order]
    sequence = [own[0], own[1], other[0], own[2], other[1], own[3], other[2], other[3]]

    def load(k):
        block, slot = sequence[k], k % 2
        row = pl.multiple_of(lax.rem(block, half) * width, width)
        from_own = lax.div(block, half) == side

        @pl.when(from_own)
        def _():
            pltpu.make_async_copy(
                key_own.at[pl.ds(row, width), :], loaded.at[slot], load_sem.at[slot]
            ).start()

        @pl.when(jnp.logical_not(from_own))
        def _():
            pltpu.make_async_copy(
                key_peer.at[pl.ds(row, width), :], loaded.at[slot], load_sem.at[slot]
            ).start()

    load(0)
    held[own[0]] = keyed[...]
    greet(z, y)

    def go_right(b):
        block = held.at[2 * b + y]
        return remote(block, block, right_sem.at[b], recv_sem.at[2 * b + y], z + 1, y)

    def go_left(b):
        block = held.at[2 * b + y]
        return remote(block, block, left_sem.at[b], recv_sem.at[2 * b + y], z - 1, y)

    def go_across(b):
        block = held.at[2 * b + y]
        return remote(block, block, across_sem.at[b], recv_sem.at[2 * b + y], z, 1 - y)

    def arrived(block):
        pltpu.make_async_copy(held.at[block], held.at[block], recv_sem.at[block]).wait()

    def forward_on(k, act):
        b = order[k]
        pl.when((b <= z) & (z < 3))(lambda: act(go_right(b)))
        pl.when((b >= z) & (z > 0))(lambda: act(go_left(b)))
        act(go_across(b))

    ones = jnp.ones((pad_rows, 128), jnp.bfloat16)
    chunk = 512

    def compute(k):
        block, slot = sequence[k], k % 2
        if k + 1 < len(sequence):
            load(k + 1)
        pltpu.make_async_copy(
            key_own.at[pl.ds(0, width), :], loaded.at[slot], load_sem.at[slot]
        ).wait()
        partial = contract_first(held[block, tokens:, :], ones)
        inner_key[...] = partial if k == 0 else inner_key[...] + partial

        @pl.loop(0, hidden // chunk)
        def _(c):
            cols = pl.ds(pl.multiple_of(c * chunk, chunk), chunk)
            product = dot(held[block, :tokens, :], loaded[slot, :, cols])
            projected[:, cols] = product if k == 0 else projected[:, cols] + product

    k = 0
    for step in range(4):
        if step > 0:
            arrived(own[step])
        forward_on(step, lambda copy: copy.start())
        compute(k)
        k += 1
        if step > 0:
            arrived(other[step - 1])
            compute(k)
            k += 1
    arrived(other[3])
    compute(k)

    factor = inner_key[...] * (noise_scale * inv_model)
    inner_key[...] = factor
    inner_value[...] = jnp.zeros_like(inner_value)

    @pl.loop(0, hidden // 128)
    def _(c):
        cols = pl.ds(pl.multiple_of(c * 128, 128), 128)
        right = key_right[:, cols].astype(jnp.float32)
        left = value_left[:, cols].astype(jnp.float32)
        for t in range(tokens // members):
            rows = slice(t * members, (t + 1) * members)
            value = projected[rows, cols] * inv_model + inner_key[rows, :] * right
            rounded = (jnp.maximum(value, 0.0) ** 2).astype(jnp.bfloat16)
            squared[rows, cols] = rounded
            inner_value[rows, :] += rounded.astype(jnp.float32) * left

    for step in range(4):
        forward_on(step, lambda copy: copy.wait_send())


def gather_key(keyed, key_own, key_peer, key_right, value_left, inv_model):
    padded, width = keyed.shape
    tokens = padded - pad_rows
    hidden = key_own.shape[1]
    slices = 8
    vmem = pl.BlockSpec(memory_space=pltpu.VMEM)
    hbm = pl.BlockSpec(memory_space=pl.ANY)
    return pl.pallas_call(
        functools.partial(gather_key_kernel, inv_model),
        out_shape=(
            jax.ShapeDtypeStruct((tokens, hidden), jnp.bfloat16),
            jax.ShapeDtypeStruct((tokens, 128), jnp.float32),
        ),
        in_specs=[vmem, hbm, hbm, vmem, vmem],
        out_specs=(vmem, vmem),
        scratch_shapes=[
            pltpu.VMEM((slices, padded, width), jnp.bfloat16),
            pltpu.VMEM((2, width, hidden), jnp.bfloat16),
            pltpu.VMEM((tokens, hidden), jnp.float32),
            pltpu.VMEM((tokens, 128), jnp.float32),
            pltpu.SemaphoreType.DMA((2,)),
            pltpu.SemaphoreType.DMA((4,)),
            pltpu.SemaphoreType.DMA((4,)),
            pltpu.SemaphoreType.DMA((4,)),
            pltpu.SemaphoreType.DMA((slices,)),
        ],
        compiler_params=pltpu.CompilerParams(
            vmem_limit_bytes=vmem_bytes, collective_id=1, has_side_effects=True
        ),
        cost_estimate=pl.CostEstimate(
            flops=16 * tokens * width * hidden,
            bytes_accessed=16 * width * hidden,
            transcendentals=0,
        ),
        name="gather_key",
    )(keyed, key_own, key_peer, key_right, value_left)


def value_scatter_kernel(
    inv_hidden, squared, inner_value, value_own, value_peer, value_right, out,
    loaded, total, inner, across, from_across, to_right, to_left, from_left, from_right,
    load_sem, across_sem, across_recv, right_sem, left_sem, left_recv, right_recv,
):
    z, y = coordinates()
    side = lax.axis_index("pop")
    rows, width = loaded.shape[1], loaded.shape[2]
    tokens = squared.shape[0]
    members = value_right.shape[0]
    half = 4
    order = [pick(z, [row[k] for row in scatter_order]) for k in range(4)]
    sequence = []
    for t in order:
        sequence += [2 * t + 1 - y, 2 * t + y]

    def load(k):
        block, slot = sequence[k], k % 2
        column = pl.multiple_of(lax.rem(block, half) * width, width)
        from_own = lax.div(block, half) == side

        @pl.when(from_own)
        def _():
            pltpu.make_async_copy(
                value_own.at[:, pl.ds(column, width)], loaded.at[slot], load_sem.at[slot]
            ).start()

        @pl.when(jnp.logical_not(from_own))
        def _():
            pltpu.make_async_copy(
                value_peer.at[:, pl.ds(column, width)], loaded.at[slot], load_sem.at[slot]
            ).start()

    load(0)
    greet(z, y)
    ones = jnp.ones((pad_rows, 128), jnp.bfloat16)
    row = jnp.zeros((pad_rows, tokens), jnp.float32)
    for term in split(inner_value[...]):
        row += lax.dot_general(
            ones, term, (((1,), (1,)), ((), ())), preferred_element_type=jnp.float32
        )

    def go_across(t):
        return remote(
            across.at[t], from_across.at[t], across_sem.at[t], across_recv.at[t], z, 1 - y
        )

    def go_right(t):
        return remote(
            to_right.at[t], from_left.at[t], right_sem.at[t], left_recv.at[t], z + 1, y
        )

    def go_left(t):
        return remote(
            to_left.at[t], from_right.at[t], left_sem.at[t], right_recv.at[t], z - 1, y
        )

    chunk = 256
    for k in range(8):
        slot, t = k % 2, order[k // 2]
        if k + 1 < 8:
            load(k + 1)
        pltpu.make_async_copy(
            value_own.at[:, pl.ds(0, width)], loaded.at[slot], load_sem.at[slot]
        ).wait()

        @pl.loop(0, width // chunk)
        def _(c):
            cols = pl.ds(pl.multiple_of(c * chunk, chunk), chunk)
            product = dot(squared[...], loaded[slot, :, cols])
            if k % 2 == 0:
                across[t, :tokens, cols] = product.astype(jnp.bfloat16)
            else:
                total[t, :, cols] = product

        if k % 2 == 0:
            across[t, tokens:, :] = as_tail(row)
            go_across(t).start()

    def take(t, arrivals, recv):
        pltpu.make_async_copy(arrivals.at[t], arrivals.at[t], recv.at[t]).wait()
        total[t] += arrivals[t, :tokens, :].astype(jnp.float32)
        inner[t] += from_tail(arrivals[t, tokens:, :])

    def put(t, departures, copy):
        departures[t, :tokens, :] = total[t].astype(jnp.bfloat16)
        departures[t, tokens:, :] = as_tail(inner[t])
        copy.start()

    for t in order:
        inner[t] = row
        take(t, from_across, across_recv)
        pl.when((t >= z) & (z > 0))(lambda: take(t, from_left, left_recv))
        pl.when((t <= z) & (z < 3))(lambda: take(t, from_right, right_recv))
        pl.when(t > z)(lambda: put(t, to_right, go_right(t)))
        pl.when(t < z)(lambda: put(t, to_left, go_left(t)))

    amount = contract_first(as_tail(inner[z]), ones) * noise_scale
    for t in range(tokens // members):
        own = slice(t * members, (t + 1) * members)
        for c in range(0, width, 128):
            cols = slice(c, c + 128)
            spread = value_right[:, cols].astype(jnp.float32)
            out[own, cols] = (
                (total[z, own, cols] + amount[own, :] * spread) * inv_hidden
            ).astype(jnp.bfloat16)

    for t in order:
        go_across(t).wait_send()
        pl.when(t > z)(lambda: go_right(t).wait_send())
        pl.when(t < z)(lambda: go_left(t).wait_send())


def value_scatter(squared, inner_value, value_own, value_peer, value_right, inv_hidden):
    tokens = squared.shape[0]
    rows = value_own.shape[0]
    width = value_right.shape[1]
    vmem = pl.BlockSpec(memory_space=pltpu.VMEM)
    hbm = pl.BlockSpec(memory_space=pl.ANY)
    message = pltpu.VMEM((4, tokens + pad_rows, width), jnp.bfloat16)
    sems = pltpu.SemaphoreType.DMA((4,))
    return pl.pallas_call(
        functools.partial(value_scatter_kernel, inv_hidden),
        out_shape=jax.ShapeDtypeStruct((tokens, width), jnp.bfloat16),
        in_specs=[vmem, vmem, hbm, hbm, vmem],
        out_specs=vmem,
        scratch_shapes=[
            pltpu.VMEM((2, rows, width), jnp.bfloat16),
            pltpu.VMEM((4, tokens, width), jnp.float32),
            pltpu.VMEM((4, pad_rows, tokens), jnp.float32),
            message, message, message, message, message, message,
            pltpu.SemaphoreType.DMA((2,)),
            sems, sems, sems, sems, sems, sems,
        ],
        compiler_params=pltpu.CompilerParams(
            vmem_limit_bytes=vmem_bytes, collective_id=2, has_side_effects=True
        ),
        cost_estimate=pl.CostEstimate(
            flops=16 * tokens * width * rows,
            bytes_accessed=16 * width * rows,
            transcendentals=0,
        ),
        name="value_scatter",
    )(squared, inner_value, value_own, value_peer, value_right)


def key_step_kernel(
    step, side_ref, left_own, left_peer, right_own, right_peer, weight, after, out_ref
):
    columns = out_ref.shape[1]
    chunk = min(512, columns)
    own, peer = left_own[0], left_peer[0]
    for c in range(0, columns, chunk):
        cols = slice(c, c + chunk)
        grad = contract_first(own, right_own[:, cols]) + contract_first(peer, right_peer[:, cols])
        out_ref[:, cols] = (weight[:, cols].astype(jnp.float32) + step * grad).astype(jnp.bfloat16)


def key_step(side, left_all, left_peer, right_own, right_peer, weight, step, after):
    half, members, width = left_peer.shape
    rows, columns = weight.shape
    fixed = pl.BlockSpec((members, columns), lambda j, s: (0, 0))
    tile = pl.BlockSpec((width, columns), lambda j, s: (j, 0))
    return pl.pallas_call(
        functools.partial(key_step_kernel, step),
        out_shape=jax.ShapeDtypeStruct(weight.shape, jnp.bfloat16),
        grid_spec=pltpu.PrefetchScalarGridSpec(
            num_scalar_prefetch=1,
            grid=(half,),
            in_specs=[
                pl.BlockSpec((1, members, width), lambda j, s: (s[0] * half + j, 0, 0)),
                pl.BlockSpec((1, members, width), lambda j, s: (j, 0, 0)),
                fixed,
                fixed,
                tile,
                pl.BlockSpec(memory_space=pl.ANY),
            ],
            out_specs=tile,
        ),
        compiler_params=pltpu.CompilerParams(vmem_limit_bytes=vmem_bytes),
        cost_estimate=pl.CostEstimate(
            flops=4 * members * rows * columns,
            bytes_accessed=4 * rows * columns + 4 * members * (rows + columns),
            transcendentals=0,
        ),
        name="key_step",
    )(side, left_all, left_peer, right_own, right_peer, weight, after)


def value_step_kernel(
    step, side_ref, left_own, left_peer, right_all, right_peer, weight, after, out_ref
):
    half, _, width = right_peer.shape
    mine = side_ref[0] * half
    own, peer = left_own[...], left_peer[...]
    for j in range(half):
        cols = slice(j * width, (j + 1) * width)
        grad = contract_first(own, right_all[mine + j]) + contract_first(peer, right_peer[j])
        out_ref[:, cols] = (weight[:, cols].astype(jnp.float32) + step * grad).astype(jnp.bfloat16)


def value_step(side, left_own, left_peer, right_all, right_peer, weight, step, after):
    half, members, width = right_peer.shape
    rows, columns = weight.shape
    size = min(512, rows)
    side_tile = pl.BlockSpec((members, size), lambda i, s: (0, i))
    tile = pl.BlockSpec((size, columns), lambda i, s: (i, 0))
    return pl.pallas_call(
        functools.partial(value_step_kernel, step),
        out_shape=jax.ShapeDtypeStruct(weight.shape, jnp.bfloat16),
        grid_spec=pltpu.PrefetchScalarGridSpec(
            num_scalar_prefetch=1,
            grid=(rows // size,),
            in_specs=[
                side_tile,
                side_tile,
                pl.BlockSpec(right_all.shape, lambda i, s: (0, 0, 0)),
                pl.BlockSpec(right_peer.shape, lambda i, s: (0, 0, 0)),
                tile,
                pl.BlockSpec(memory_space=pl.ANY),
            ],
            out_specs=tile,
        ),
        compiler_params=pltpu.CompilerParams(vmem_limit_bytes=vmem_bytes),
        cost_estimate=pl.CostEstimate(
            flops=4 * members * rows * columns,
            bytes_accessed=4 * rows * columns + 4 * members * (rows + columns),
            transcendentals=0,
        ),
        name="value_step",
    )(side, left_own, left_peer, right_all, right_peer, weight, after)


def shards(
    token_ids, ranks, embedding, mix_key, key_weight, value_weight,
    key_left, key_right, value_left, value_right,
):
    members = ranks.shape[0]
    population = members * lax.axis_size("pop")
    side = lax.axis_index("pop")
    side_ref = side.astype(jnp.int32).reshape(1)
    slices = lax.axis_size("mp")
    half = slices // 2
    width = embedding.shape[1]
    model = slices * width
    hidden = slices * key_weight.shape[1]
    swap = lambda array: lax.ppermute(array, "pop", [(0, 1), (1, 0)])

    half_vocab = embedding.shape[0]
    by_side = jnp.swapaxes(token_ids.reshape(2, members, 2), 1, 2)

    tokens = 2 * members
    ids = jnp.concatenate(
        [
            lax.dynamic_index_in_dim(by_side, side, 0, keepdims=False).reshape(-1),
            lax.dynamic_index_in_dim(by_side, 1 - side, 0, keepdims=False).reshape(-1),
        ]
    )
    ids = ids - side * half_vocab
    inside = (ids[:tokens] >= 0) & (ids[:tokens] < half_vocab)
    looked = jnp.take(embedding, jnp.clip(ids, 0, half_vocab - 1), axis=0, mode="clip")
    received = swap(looked[tokens:])
    rows = jnp.where(inside[:, None], looked[:tokens], received).astype(jnp.float32)
    first, second = rows[:members], rows[members:]
    keyed = jnp.concatenate(
        [first + (0.0 - first) * mix_key, second + (first - second) * mix_key], axis=0
    ).astype(jnp.bfloat16)
    left = key_left.astype(jnp.float32)
    inner = jnp.sum(
        keyed.astype(jnp.float32).reshape(2, members, width) * left[None], axis=2
    ).reshape(-1)
    groups = -(-2 * members // width)
    tail = jnp.stack(split(inner)).reshape(3 * groups, width)
    tail = jnp.pad(tail, ((0, pad_rows - 3 * groups), (0, 0)))
    keyed = jnp.concatenate([keyed, tail], axis=0)
    right_all = lax.all_gather(value_right, "mp", axis=0)
    key_peer, value_peer = swap(key_weight), swap(value_weight)
    if slices == 8 and 2 * members == width:
        squared, inner_value = gather_key(
            keyed, key_weight, key_peer, key_right, value_left, model ** -0.5
        )
        right_all, later_left, squared = lax.optimization_barrier((right_all, key_left, squared))
        left_all = lax.all_gather(later_left, "mp", axis=0)
        mixed = value_scatter(
            squared, inner_value, value_weight, value_peer, value_right, hidden ** -0.5
        )
        left_all, mixed = lax.optimization_barrier((left_all, mixed))
    else:
        left_all = lax.all_gather(key_left, "mp", axis=0)
        partial = forward(
            side_ref, lax.all_gather(keyed, "mp", axis=0), key_weight, key_peer, value_weight,
            value_peer, key_right, value_left, right_all, model ** -0.5, hidden ** -0.5,
        )
        mixed = lax.psum_scatter(partial, "mp", scatter_dimension=0, tiled=False)
    summed = mixed
    mixed = jnp.swapaxes(mixed.reshape(2, members, width), 0, 1).reshape(2 * members, width)

    fitness = (2 * ranks - (population - 1)).astype(jnp.float32) / (population - 1)
    scaled_right = (fitness[:, None] * key_right.astype(jnp.float32)).astype(jnp.bfloat16)
    scaled_left = (fitness[:, None] * value_left.astype(jnp.float32)).astype(jnp.bfloat16)
    other = (1 - side) * half
    left_peer = swap(lax.dynamic_slice_in_dim(left_all, other, half, 0))
    right_peer = swap(lax.dynamic_slice_in_dim(right_all, other, half, 0))
    step = step_scale / population
    new_key = key_step(
        side_ref, left_all, left_peer, scaled_right, swap(scaled_right), key_weight, step,
        summed,
    )
    new_value = value_step(
        side_ref, scaled_left, swap(scaled_left), right_all, right_peer, value_weight, step,
        summed,
    )
    return (mixed, new_key, new_value)


def solution(mesh):
    placed = (
        P("grp", None),
        P(("grp", "pop")),
        P("pop", "mp"),
        P("mp"),
        P("pop", "mp"),
        P("mp", "pop"),
        P(("grp", "pop"), "mp"),
        P(("grp", "pop"), "mp"),
        P(("grp", "pop"), "mp"),
        P(("grp", "pop"), "mp"),
    )
    return jax.shard_map(
        shards,
        mesh=mesh,
        in_specs=placed,
        out_specs=(P(("grp", "pop"), "mp"), P(("grp", "pop"), "mp"), P(("grp", "mp"), "pop")),
        check_vma=False,
    )
```
